128 devices in a mesh: blk: 32 (over y, x, z_lo), rep: 4 (over z_hi, core).
Axes of the slice: x: 4, y: 4, z: 4 (z_hi: 2, z_lo: 2; z = z_hi * 2 + z_lo), core: 2. Of those that a mesh axis runs over, the one named last changes fastest.
Arguments:
- features: bfloat16 [32768, 256], P('blk'), may hold values from -6 to 6
- tiles: bfloat16 [256, 32, 6, 128, 128], P('blk', 'rep'), may hold values from -0.375 to 0.375
- tile_cols: int32 [256, 32, 6], P('blk', 'rep'), may hold values from 0 to 7
- counts: int32 [256, 32], P('blk', 'rep'), may hold values from 0 to 6
- degree: int32 [32768], P('blk'), may hold values from 1 to 16
- train_mask: int32 [32768], P('blk'), may hold values 0 or 1
- cotangent: bfloat16 [32768, 256], P('blk'), may hold values from -6 to 6
- w_self: bfloat16 [256, 256], replicated, may hold values from -0.375 to 0.375
- w_neigh: bfloat16 [256, 256], replicated, may hold values from -0.375 to 0.375
- bias_term: float32 [256], replicated, may hold values from -3 to 3
Outputs:
- activation: bfloat16 [32768, 256], P(('blk', 'rep'))
- grad_features: bfloat16 [32768, 256], P(('blk', 'rep'))
- grad_self: float32 [256, 256], replicated
- grad_neigh: float32 [256, 256], replicated
- grad_bias: float32 [256], replicated
The draws below stay inside these ranges and needn't reach their ends.
Inputs may be any that keep to these rules, and one draw needn't show every extreme that they name: `tile_cols`: a column block index inside the owner's 8 blocks. `counts`: tiles at positions of count or more are ignored.
All inputs are finite; a program needn't handle non-finite values. No bound on the sum of `train_mask` on one device may be relied on, other than what follows from the above.
Results may differ from the reference program's by a relative error of at most 0.0075.
Values may be sent and summed in bfloat16 or wider, within the bound.
No kernel may reach another device: no remote copies, remote signals or barrier semaphores. Data moves between devices by JAX's collectives and lax.ppermute only.
A program may use at most 128 MiB of HBM per device.

```python
import jax
import jax.numpy as jnp
from jax import lax

F = 256
BS = 128
SLOTS = 6
NB_DEV = 8
ROW_BLOCKS = 256
NODES = 32768
N_BLK = 32


def touch_ends(values, own_key, low, top_value):
    longest = values.shape.index(max(values.shape))
    spots = []
    for shift in (0, 1):
        where = [jax.random.randint(jax.random.fold_in(own_key, axis), (), 0, length) for axis, length in enumerate(values.shape)]
        where[longest] = (where[longest] + shift) % values.shape[longest]
        spots.append(tuple(where))
    return values.at[spots[0]].set(low).at[spots[1]].set(top_value)


def block_levels(stream_key, extent, shards, smallest, top_value):
    def one(position, parts):
        draws = jax.random.uniform(jax.random.fold_in(jax.random.fold_in(stream_key, 6), position), (parts,), jnp.float32, smallest / len(shards), top_value / len(shards))
        return jnp.repeat(jnp.exp(draws), extent[position] // parts).reshape((-1,) + (1,) * (len(extent) - position - 1))

    factor_of = one(*shards[0])
    for cut in shards[1:]:
        factor_of = factor_of * one(*cut)
    return factor_of


def centred(key, shape, width, limit, pieces=(), kind=jnp.bfloat16):
    entries = jax.random.normal(key, shape, jnp.float32) * width
    if len(pieces) > 0:
        entries = block_levels(key, shape, pieces, -0.22, 0.18) * entries
    return jnp.clip(entries, min=-limit, max=limit).astype(kind)


def setup_inputs(seed: int = 0) -> dict:
    arg_keys = jax.random.split(jax.random.key(seed), 11)
    return {
        "features": centred(arg_keys[0], (NODES, F), 1.0, 6.0, ((0, 32),)),
        "tiles": centred(arg_keys[1], (ROW_BLOCKS, N_BLK, SLOTS, BS, BS), (3.0 * (BS * N_BLK * SLOTS // 2) ** -0.5), 0.375, ((0, 32), (1, 4))),
        "tile_cols": touch_ends(jax.random.randint(arg_keys[2], (ROW_BLOCKS, N_BLK, SLOTS), 0, NB_DEV), jax.random.fold_in(arg_keys[2], 1), 0, NB_DEV - 1).astype(jnp.int32),
        "counts": touch_ends(jax.random.randint(arg_keys[3], (ROW_BLOCKS, N_BLK), 0, SLOTS + 1), jax.random.fold_in(arg_keys[3], 1), 0, SLOTS).astype(jnp.int32),
        "degree": touch_ends(jax.random.randint(arg_keys[4], (NODES,), 1, 17), jax.random.fold_in(arg_keys[4], 1), 1, 16).astype(jnp.int32),
        "train_mask": touch_ends((jax.random.randint(arg_keys[5], (NODES,), 0, 2) < 1).astype(jnp.int32), jax.random.fold_in(arg_keys[5], 1), 0, 1),
        "cotangent": centred(arg_keys[6], (NODES, F), 1.0, 6.0, ((0, 32),)),
        "w_self": centred(arg_keys[7], (F, F), F ** -0.5, 0.375),
        "w_neigh": centred(arg_keys[8], (F, F), F ** -0.5, 0.375),
        "bias_term": centred(arg_keys[9], (F,), 0.5, 3.0, (), jnp.float32),
    }


def dense_rows(own_rows, aggregate, cot_rows, mask_rows, w_self, w_neigh, bias_term):
    pre_act = jnp.dot(own_rows, w_self, preferred_element_type=jnp.float32) + jnp.dot(aggregate, w_neigh, preferred_element_type=jnp.float32) + bias_term
    sigm = jax.nn.sigmoid(pre_act)
    activation = (pre_act * sigm).astype(jnp.bfloat16)
    slope = sigm * (1.0 + pre_act * (1.0 - sigm))
    grad_pre = (mask_rows.astype(jnp.float32)[:, None] * cot_rows.astype(jnp.float32) * slope).astype(jnp.bfloat16)
    return (activation, grad_pre)

def reference(features, tiles, tile_cols, counts, degree, train_mask, cotangent, w_self, w_neigh, bias_term):
    row_blocks = NB_DEV * N_BLK
    owners = (jnp.arange(row_blocks, dtype=jnp.int32) // NB_DEV).astype(jnp.int32)
    slot_ids = jnp.arange(SLOTS, dtype=jnp.int32)
    feat_blocks = features.reshape(row_blocks, BS, F).astype(jnp.float32)

    def pick(distance):
        tile_now = lax.dynamic_index_in_dim(tiles, distance, 1, keepdims=False).astype(jnp.float32)
        col_now = lax.dynamic_index_in_dim(tile_cols, distance, 1, keepdims=False)
        count_now = lax.dynamic_index_in_dim(counts, distance, 1, keepdims=False)
        target = ((owners - distance) % N_BLK * NB_DEV)[:, None] + col_now
        live_slots = (slot_ids[None, :] < count_now[:, None]).astype(jnp.float32)
        return (tile_now, target.astype(jnp.int32), live_slots)

    def forward_step(running, distance):
        tile_now, target, live_slots = pick(distance)
        picked = feat_blocks[target] * live_slots[:, :, None, None]
        return (running + jnp.einsum('rsij,rsjf->rif', tile_now, picked, precision=lax.Precision.HIGHEST), None)
    distances = jnp.arange(N_BLK, dtype=jnp.int32)
    partial_value, _ = lax.scan(forward_step, jnp.zeros((row_blocks, BS, F), jnp.float32), distances)
    inv_degree = 1.0 / degree.astype(jnp.float32)
    aggregate = (partial_value.reshape(NODES, F) * inv_degree[:, None]).astype(jnp.bfloat16)
    activation, grad_pre = dense_rows(features, aggregate, cotangent, train_mask, w_self, w_neigh, bias_term)
    norm_factor = 1.0 / jnp.sqrt(jnp.float32(NODES))
    grad_f32 = grad_pre.astype(jnp.float32)
    grad_self = jnp.einsum('nf,ng->fg', features.astype(jnp.float32), grad_f32, precision=lax.Precision.HIGHEST) * norm_factor
    grad_neigh = jnp.einsum('nf,ng->fg', aggregate.astype(jnp.float32), grad_f32, precision=lax.Precision.HIGHEST) * norm_factor
    grad_bias = lax.optimization_barrier(jnp.sum(grad_f32, axis=0)) * norm_factor
    back_msg = (jnp.dot(grad_pre, w_neigh.T, preferred_element_type=jnp.float32) * inv_degree[:, None]).astype(jnp.bfloat16)
    back_blocks = back_msg.reshape(row_blocks, BS, F).astype(jnp.float32)

    def backward_step(running, distance):
        tile_now, target, live_slots = pick(distance)
        products = jnp.einsum('rsji,rjf->rsif', tile_now, back_blocks, precision=lax.Precision.HIGHEST)
        products = products * live_slots[:, :, None, None]
        return (running.at[target].add(products), None)
    spread, _ = lax.scan(backward_step, jnp.zeros((row_blocks, BS, F), jnp.float32), distances)
    own_term = jnp.dot(grad_pre, w_self.T, preferred_element_type=jnp.float32)
    grad_features = (own_term + spread.reshape(NODES, F)).astype(jnp.bfloat16)
    return (activation, grad_features, grad_self, grad_neigh, grad_bias)
```

```python
import functools

import jax
import jax.numpy as jnp
from jax import lax
from jax.experimental import pallas as pl
from jax.experimental.pallas import tpu as pltpu
from jax.sharding import PartitionSpec as P

AXES = ("blk", "rep")
NB = 8
ND = 8
NS = 6
BS = 128
F = 256
VMEM = 40 * 1024 * 1024
PLAN = ((2, None), (6, None), (3, None), (7, None), (1, None), (0, None), (4, 2), (5, 6))


def index_of(y, x, zl, zh, core):
    return (((y % 4 * 4 + x % 4) * 2 + zl) * 2 + zh) * 2 + core


def places():
    for t in range(128):
        yield t, t >> 5, t >> 3 & 3, t >> 2 & 1, t >> 1 & 1, t & 1


def column_pairs(k, via):
    out = []
    for t, y, x, zl, zh, core in places():
        j, r = x * 2 + zl, 2 * zh + core
        jj = j ^ k
        if via is None:
            out.append((index_of(y - r - (jj > j), jj >> 1, jj & 1, zh ^ (k & 1), core), t))
        else:
            jn = j ^ via
            out.append((index_of(y - (jj > j) + (jj > jn), jn >> 1, jn & 1, zh, core), t))
    return out


def flip_pairs(dy=0, dx=0, dzl=0, dzh=0, dcore=0):
    return [
        (t, index_of(y ^ dy, x ^ dx, zl ^ dzl, zh ^ dzh, core ^ dcore))
        for t, y, x, zl, zh, core in places()
    ]


def send(value, pairs):
    return lax.ppermute(value, AXES, pairs)


def back(pairs):
    return [(b, a) for a, b in pairs]


def params():
    return pltpu.CompilerParams(vmem_limit_bytes=VMEM)


def forward_body(first, sel_ref, cols_ref, counts_ref, tiles_ref, shard_ref, *rest):
    out_ref = rest[-1]
    step = pl.program_id(0)
    dist = sel_ref[0]
    for inner in range(2):
        b = step * 2 + inner
        count = counts_ref[b * ND + dist]
        left, right = [], []
        for s in range(NS):
            col = cols_ref[(b * ND + dist) * NS + s]
            block = shard_ref[pl.ds(pl.multiple_of(col * BS, BS), BS), :]
            right.append(jnp.where(s < count, block, jnp.zeros((), block.dtype)))
            left.append(tiles_ref[inner, 0, s])
        summed = jnp.dot(
            jnp.concatenate(left, 1), jnp.concatenate(right, 0), preferred_element_type=jnp.float32
        )
        rows = pl.ds(pl.multiple_of(b * BS, BS), BS)
        if first:
            out_ref[rows, :] = summed
        else:
            out_ref[rows, :] = rest[0][rows, :] + summed


def forward_call(dist, cols, counts, tiles, shard, total):
    first = total is None
    whole = pl.BlockSpec((NB * BS, F), lambda i, *_: (0, 0))
    in_specs = [
        pl.BlockSpec((2, 1, NS, BS, BS), lambda i, sel, c, n: (i, sel[0], 0, 0, 0)),
        whole,
    ] + ([] if first else [whole])
    return pl.pallas_call(
        functools.partial(forward_body, first),
        out_shape=jax.ShapeDtypeStruct((NB * BS, F), jnp.float32),
        grid_spec=pltpu.PrefetchScalarGridSpec(
            num_scalar_prefetch=3, grid=(NB // 2,), in_specs=in_specs, out_specs=whole
        ),
        compiler_params=params(),
        name="forward_tiles",
    )(dist, cols, counts, tiles, shard, *([] if first else [total]))


def dense_body(
    rep_ref, own_ref, got_ref, feat_ref, cot_ref, mask_ref, inv_ref, invt_ref, ws_ref, wn_ref,
    bias_ref, act_ref, term_ref, back_ref, grad_ref, sums_ref,
):
    rep = rep_ref[0]
    zh, core = rep // 2, rep % 2
    nt = (((1,), (1,)), ((), ()))
    tn = (((0,), (0,)), ((), ()))
    grads = jnp.zeros((F, F), jnp.float32)
    sums = jnp.zeros((1, F), jnp.float32)
    for part in range(2):
        quarter = part * 2 + core
        rows = pl.ds(pl.multiple_of(quarter * 256, 256), 256)
        feat = feat_ref[rows, :]
        summed = own_ref[part].astype(jnp.float32) + got_ref[part].astype(jnp.float32)
        agg = (summed * inv_ref[rows, :]).astype(jnp.bfloat16)
        pre = (
            jnp.dot(feat, ws_ref[...], preferred_element_type=jnp.float32)
            + jnp.dot(agg, wn_ref[...], preferred_element_type=jnp.float32)
            + bias_ref[...]
        )
        sigm = jax.nn.sigmoid(pre)
        act = (pre * sigm).astype(jnp.bfloat16)
        slope = sigm * (1.0 + pre * (1.0 - sigm))
        grad_pre = (mask_ref[rows, :] * cot_ref[rows, :].astype(jnp.float32) * slope).astype(
            jnp.bfloat16
        )

        @pl.when(zh == part)
        def _():
            act_ref[...] = act
            term_ref[...] = lax.dot_general(
                grad_pre, ws_ref[...], nt, preferred_element_type=jnp.float32
            )

        back_t = lax.dot_general(wn_ref[...], grad_pre, nt, preferred_element_type=jnp.float32)
        back_ref[part] = (back_t * invt_ref[quarter]).astype(jnp.bfloat16)
        left = jnp.where(zh == 0, feat, agg)
        grads += lax.dot_general(left, grad_pre, tn, preferred_element_type=jnp.float32)
        sums += jnp.sum(grad_pre.astype(jnp.float32), axis=0, keepdims=True)
    grad_ref[...] = grads
    sums_ref[...] = sums


def dense_call(rep, own, got, feat, cot, mask, inv, inv_t, w_self, w_neigh, bias):
    vmem = pl.BlockSpec(memory_space=pltpu.VMEM)
    return pl.pallas_call(
        dense_body,
        out_shape=(
            jax.ShapeDtypeStruct((256, F), jnp.bfloat16),
            jax.ShapeDtypeStruct((256, F), jnp.float32),
            jax.ShapeDtypeStruct((2, F, 256), jnp.bfloat16),
            jax.ShapeDtypeStruct((F, F), jnp.float32),
            jax.ShapeDtypeStruct((1, F), jnp.float32),
        ),
        in_specs=[pl.BlockSpec(memory_space=pltpu.SMEM)] + [vmem] * 10,
        out_specs=(vmem,) * 5,
        compiler_params=params(),
        name="dense_rows",
    )(rep, own, got, feat, cot, mask, inv, inv_t, w_self, w_neigh, bias)


def backward_body(added, sel_ref, cols_ref, counts_ref, tiles_ref, own_ref, got_ref, *rest):
    out_ref, acc_ref = rest[-2:]
    step = pl.program_id(0)
    dist = sel_ref[0]
    core = sel_ref[1]

    @pl.when(step == 0)
    def _():
        for c in range(NB):
            if added:
                acc_ref[c] = rest[0][c].astype(jnp.float32)
            else:
                acc_ref[c] = jnp.zeros((F, BS), jnp.float32)

    mine = step % 2 == core
    part = step // 2
    message = jnp.where(mine, own_ref[part], got_ref[part])
    for inner in range(2):
        b = step * 2 + inner
        count = counts_ref[b * ND + dist]
        left = message[:, inner * BS : (inner + 1) * BS]
        for s in range(0, NS, 2):
            right = jnp.concatenate([tiles_ref[inner, 0, s], tiles_ref[inner, 0, s + 1]], 1)
            product = jnp.dot(left, right, preferred_element_type=jnp.float32)
            for k in range(2):
                col = cols_ref[(b * ND + dist) * NS + s + k]
                col = jnp.where(s + k < count, col, NB)
                acc_ref[col] += product[:, k * BS : (k + 1) * BS]

    @pl.when(step == NB // 2 - 1)
    def _():
        for c in range(NB):
            out_ref[c] = acc_ref[c].astype(jnp.bfloat16)


def backward_call(sel, cols, counts, tiles, own, got, extra):
    added = extra is not None
    whole = pl.BlockSpec((NB, F, BS), lambda i, *_: (0, 0, 0))
    message = pl.BlockSpec((2, F, 256), lambda i, *_: (0, 0, 0))
    in_specs = [
        pl.BlockSpec((2, 1, NS, BS, BS), lambda i, sel, c, n: (i, sel[0], 0, 0, 0)),
        message,
        message,
    ] + ([whole] if added else [])
    return pl.pallas_call(
        functools.partial(backward_body, added),
        out_shape=jax.ShapeDtypeStruct((NB, F, BS), jnp.bfloat16),
        grid_spec=pltpu.PrefetchScalarGridSpec(
            num_scalar_prefetch=3,
            grid=(NB // 2,),
            in_specs=in_specs,
            out_specs=whole,
            scratch_shapes=[pltpu.VMEM((NB + 1, F, BS), jnp.float32)],
        ),
        compiler_params=params(),
        name="backward_tiles",
    )(sel, cols, counts, tiles, own, got, *([extra] if added else []))


def final_body(kept_ref, got_ref, term_ref, out_ref):
    for c in range(2):
        spread = kept_ref[c] + got_ref[c].astype(jnp.float32)
        rows = slice(c * BS, (c + 1) * BS)
        out_ref[rows, :] = (term_ref[rows, :] + spread.T).astype(jnp.bfloat16)


def final_call(kept, got, term):
    return pl.pallas_call(
        final_body,
        out_shape=jax.ShapeDtypeStruct((256, F), jnp.bfloat16),
        compiler_params=params(),
        name="final_rows",
    )(kept, got, term)


def pick(pair, index):
    return lax.dynamic_index_in_dim(pair, index, 0, keepdims=False)


def summed_over(value, flips):
    value = value.astype(jnp.bfloat16)
    got = [send(value, flip_pairs(**f)).astype(jnp.float32) for f in flips]
    value = value.astype(jnp.float32)
    if len(got) == 1:
        return value + got[0]
    return (value + got[0]) + (got[1] + got[2])


def weight_grads(grads, sums, zh, core, nodes):
    halves = grads.reshape(2, F // 2, F)
    mine = pick(halves, core) + send(pick(halves, 1 - core), flip_pairs(dcore=1))
    bias = sums + send(sums, flip_pairs(dcore=1))
    high = bias.astype(jnp.bfloat16).astype(jnp.float32)
    pad = jnp.zeros((14, F), jnp.float32)
    value = jnp.concatenate([mine, high, bias - high, pad], 0)

    def split_bias(v):
        total = v[F // 2 : F // 2 + 1] + v[F // 2 + 1 : F // 2 + 2]
        hi = total.astype(jnp.bfloat16).astype(jnp.float32)
        return jnp.concatenate([v[: F // 2], hi, total - hi, pad], 0)

    value = split_bias(summed_over(value, [dict(dy=1), dict(dy=2), dict(dy=3)]))
    value = split_bias(summed_over(value, [dict(dx=1), dict(dx=2), dict(dx=3)]))
    value = summed_over(value, [dict(dzl=1)])
    bias = value[F // 2] + value[F // 2 + 1]
    half = value[: F // 2]
    other = send(half, flip_pairs(dzh=1))
    both = jnp.where(zh == 0, jnp.stack([half, other]), jnp.stack([other, half]))
    across = send(both, flip_pairs(dcore=1))
    low, top = jnp.where(core == 0, both, across), jnp.where(core == 0, across, both)
    norm = 1.0 / jnp.sqrt(jnp.float32(nodes))
    whole = jnp.concatenate([low, top], 1) * norm
    return whole[0], whole[1], bias * norm


def shards(
    features, tiles, tile_cols, counts, degree, train_mask, cotangent, w_self, w_neigh, bias_term
):
    rows = features.shape[0]
    rep = lax.axis_index("rep").astype(jnp.int32)
    zh, core = rep // 2, rep % 2
    place = (lax.axis_index("blk") % 8).astype(jnp.int32)
    cols = tile_cols.reshape(-1)
    live = counts.reshape(-1)

    def distance_of(k):
        return (place - (place ^ k)) % 8

    inv = 1.0 / degree.astype(jnp.float32)
    inv_col = inv.reshape(rows, 1)
    inv_row = inv.reshape(4, 1, 256)
    mask = train_mask.astype(jnp.float32).reshape(rows, 1)
    bias = bias_term.reshape(1, F)

    blocks = {}
    total = None
    for k, via in PLAN:
        source = features if via is None else blocks[k ^ via]
        blocks[k] = send(source, column_pairs(k, via))
    for k, _ in PLAN:
        total = forward_call(distance_of(k)[None], cols, live, tiles, blocks[k], total)

    parts = total.reshape(2, 2, 256, F)
    away = lax.dynamic_index_in_dim(parts, 1 - core, 1, keepdims=False).astype(jnp.bfloat16)
    kept = lax.dynamic_index_in_dim(parts, core, 1, keepdims=False)
    chip = (kept + send(away, flip_pairs(dcore=1)).astype(jnp.float32)).astype(jnp.bfloat16)
    other = send(chip, flip_pairs(dzh=1))

    activation, own_term, back_own, grads, sums = dense_call(
        rep[None], chip, other, features, cotangent, mask, inv_col, inv_row, w_self, w_neigh, bias
    )
    back_got = send(back_own, flip_pairs(dcore=1))

    grad_self, grad_neigh, grad_bias = weight_grads(
        grads, sums, zh, core, rows * lax.axis_size("blk")
    )

    extra = {}
    arrived = None
    for k, via in reversed(PLAN):
        sel = jnp.stack([distance_of(k), core])
        made = backward_call(sel, cols, live, tiles, back_own, back_got, extra.get(k))
        moved = send(made, back(column_pairs(k, via)))
        if via is None:
            moved = moved.astype(jnp.float32)
            arrived = moved if arrived is None else arrived + moved
        else:
            extra[k ^ via] = moved

    parts = arrived.reshape(2, 2, 2, F, BS)
    away = lax.dynamic_index_in_dim(parts, 1 - core, 1, keepdims=False).astype(jnp.bfloat16)
    kept = lax.dynamic_index_in_dim(parts, core, 1, keepdims=False)
    chip = kept + send(away, flip_pairs(dcore=1)).astype(jnp.float32)
    got = send(pick(chip, 1 - zh).astype(jnp.bfloat16), flip_pairs(dzh=1))
    grad_features = final_call(pick(chip, zh), got, own_term)
    return (activation, grad_features, grad_self, grad_neigh, grad_bias)


def solution(mesh):
    return jax.shard_map(
        shards,
        mesh=mesh,
        in_specs=(
            P("blk", None),
            P("blk", "rep", None, None, None),
            P("blk", "rep", None),
            P("blk", "rep"),
            P("blk"),
            P("blk"),
            P("blk", None),
            P(),
            P(),
            P(),
        ),
        out_specs=(P(("blk", "rep"), None), P(("blk", "rep"), None), P(), P(), P()),
        check_vma=False,
    )
```

```python
import functools

import jax
import jax.numpy as jnp
from jax import lax
from jax.experimental import pallas as pl
from jax.experimental.pallas import tpu as pltpu
from jax.sharding import PartitionSpec as P

AXES = ("blk", "rep")
NB = 8
ND = 8
NS = 6
BS = 128
F = 256
VMEM = 40 * 1024 * 1024
PLAN = ((2, None), (6, None), (3, None), (7, None), (1, None), (0, None), (4, 2), (5, 6))


def index_of(y, x, zl, zh, core):
    return (((y % 4 * 4 + x % 4) * 2 + zl) * 2 + zh) * 2 + core


def places():
    for t in range(128):
        yield t, t >> 5, t >> 3 & 3, t >> 2 & 1, t >> 1 & 1, t & 1


def column_pairs(k, via):
    out = []
    for t, y, x, zl, zh, core in places():
        j, r = x * 2 + zl, 2 * zh + core
        jj = j ^ k
        if via is None:
            out.append((index_of(y - r - (jj > j), jj >> 1, jj & 1, zh ^ (k & 1), core), t))
        else:
            jn = j ^ via
            out.append((index_of(y - (jj > j) + (jj > jn), jn >> 1, jn & 1, zh, core), t))
    return out


def flip_pairs(dy=0, dx=0, dzl=0, dzh=0, dcore=0):
    return [
        (t, index_of(y ^ dy, x ^ dx, zl ^ dzl, zh ^ dzh, core ^ dcore))
        for t, y, x, zl, zh, core in places()
    ]


def send(value, pairs):
    return lax.ppermute(value, AXES, pairs)


def back(pairs):
    return [(b, a) for a, b in pairs]


def params():
    return pltpu.CompilerParams(vmem_limit_bytes=VMEM)


def load_tiles(tiles_ref, dist, held_ref, sems):
    copies = [
        pltpu.make_async_copy(tiles_ref.at[b, dist], held_ref.at[b], sems.at[b]) for b in range(NB)
    ]
    for copy in copies:
        copy.start()
    return copies


def tile_scratch():
    return [pltpu.VMEM((NB, NS, BS, BS), jnp.bfloat16), pltpu.SemaphoreType.DMA((NB,))]


def tile_cost():
    return pl.CostEstimate(
        flops=2 * NB * NS * BS * BS * F, bytes_accessed=8 << 20, transcendentals=0
    )


SMEM = pl.BlockSpec(memory_space=pltpu.SMEM)
HBM = pl.BlockSpec(memory_space=pltpu.HBM)
WHOLE = pl.BlockSpec(memory_space=pltpu.VMEM)


def forward_body(first, sel_ref, cols_ref, counts_ref, tiles_ref, shard_ref, *rest):
    out_ref, held_ref, sems = rest[-3:]
    dist = sel_ref[0]
    copies = load_tiles(tiles_ref, dist, held_ref, sems)
    for b in range(NB):
        copies[b].wait()
        count = counts_ref[b * ND + dist]
        rows = slice(b * BS, (b + 1) * BS)
        out_ref[rows, :] = jnp.zeros((BS, F), jnp.float32) if first else rest[0][rows, :]
        for s in range(0, NS, 2):

            @pl.when(s < count)
            def _():
                left, right = [], []
                for k in range(s, s + 2):
                    col = cols_ref[(b * ND + dist) * NS + k]
                    block = shard_ref[pl.ds(pl.multiple_of(col * BS, BS), BS), :]
                    if k > s:
                        block = jnp.where(k < count, block, jnp.zeros((), block.dtype))
                    right.append(block)
                    left.append(held_ref[b, k])
                out_ref[rows, :] += jnp.dot(
                    jnp.concatenate(left, 1),
                    jnp.concatenate(right, 0),
                    preferred_element_type=jnp.float32,
                )


def forward_call(dist, cols, counts, tiles, shard, total):
    first = total is None
    return pl.pallas_call(
        functools.partial(forward_body, first),
        out_shape=jax.ShapeDtypeStruct((NB * BS, F), jnp.float32),
        in_specs=[SMEM] * 3 + [HBM, WHOLE] + ([] if first else [WHOLE]),
        out_specs=WHOLE,
        scratch_shapes=tile_scratch(),
        compiler_params=params(),
        cost_estimate=tile_cost(),
        name="forward_tiles",
    )(dist, cols, counts, tiles, shard, *([] if first else [total]))


def dense_body(
    rep_ref, own_ref, got_ref, feat_ref, cot_ref, mask_ref, inv_ref, invt_ref, ws_ref, wn_ref,
    bias_ref, act_ref, term_ref, back_ref, grad_ref, sums_ref,
):
    rep = rep_ref[0]
    zh, core = rep // 2, rep % 2
    nt = (((1,), (1,)), ((), ()))
    tn = (((0,), (0,)), ((), ()))
    grads = jnp.zeros((F, F), jnp.float32)
    sums = jnp.zeros((1, F), jnp.float32)
    for part in range(2):
        quarter = part * 2 + core
        rows = pl.ds(pl.multiple_of(quarter * 256, 256), 256)
        feat = feat_ref[rows, :]
        summed = own_ref[part].astype(jnp.float32) + got_ref[part].astype(jnp.float32)
        agg = (summed * inv_ref[rows, :]).astype(jnp.bfloat16)
        pre = (
            jnp.dot(feat, ws_ref[...], preferred_element_type=jnp.float32)
            + jnp.dot(agg, wn_ref[...], preferred_element_type=jnp.float32)
            + bias_ref[...]
        )
        sigm = jax.nn.sigmoid(pre)
        act = (pre * sigm).astype(jnp.bfloat16)
        slope = sigm * (1.0 + pre * (1.0 - sigm))
        grad_pre = (mask_ref[rows, :] * cot_ref[rows, :].astype(jnp.float32) * slope).astype(
            jnp.bfloat16
        )

        @pl.when(zh == part)
        def _():
            act_ref[...] = act
            term_ref[...] = lax.dot_general(
                grad_pre, ws_ref[...], nt, preferred_element_type=jnp.float32
            )

        back_t = lax.dot_general(wn_ref[...], grad_pre, nt, preferred_element_type=jnp.float32)
        back_ref[part] = (back_t * invt_ref[quarter]).astype(jnp.bfloat16)
        left = jnp.where(zh == 0, feat, agg)
        grads += lax.dot_general(left, grad_pre, tn, preferred_element_type=jnp.float32)
        sums += jnp.sum(grad_pre.astype(jnp.float32), axis=0, keepdims=True)
    grad_ref[...] = grads
    sums_ref[...] = sums


def dense_call(rep, own, got, feat, cot, mask, inv, inv_t, w_self, w_neigh, bias):
    vmem = pl.BlockSpec(memory_space=pltpu.VMEM)
    return pl.pallas_call(
        dense_body,
        out_shape=(
            jax.ShapeDtypeStruct((256, F), jnp.bfloat16),
            jax.ShapeDtypeStruct((256, F), jnp.float32),
            jax.ShapeDtypeStruct((2, F, 256), jnp.bfloat16),
            jax.ShapeDtypeStruct((F, F), jnp.float32),
            jax.ShapeDtypeStruct((1, F), jnp.float32),
        ),
        in_specs=[pl.BlockSpec(memory_space=pltpu.SMEM)] + [vmem] * 10,
        out_specs=(vmem,) * 5,
        compiler_params=params(),
        name="dense_rows",
    )(rep, own, got, feat, cot, mask, inv, inv_t, w_self, w_neigh, bias)


def backward_body(
    added, passed, sel_ref, cols_ref, counts_ref, tiles_ref, own_ref, got_ref, *rest
):
    acc_ref, held_ref, sems = rest[-3:]
    out_ref = rest[added + passed]
    dist, core = sel_ref[0], sel_ref[1]
    copies = load_tiles(tiles_ref, dist, held_ref, sems)
    for c in range(NB):
        if added:
            acc_ref[c] = rest[0][c].astype(jnp.float32)
        else:
            acc_ref[c] = jnp.zeros((F, BS), jnp.float32)
    for quarter in range(NB // 2):
        mine = core == quarter % 2
        message = jnp.where(mine, own_ref[quarter // 2], got_ref[quarter // 2])
        for inner in range(2):
            b = quarter * 2 + inner
            copies[b].wait()
            count = counts_ref[b * ND + dist]
            left = message[:, inner * BS : (inner + 1) * BS]
            for s in range(0, NS, 2):

                @pl.when(s < count)
                def _():
                    right = jnp.concatenate([held_ref[b, s], held_ref[b, s + 1]], 1)
                    product = jnp.dot(left, right, preferred_element_type=jnp.float32)
                    for k in range(2):
                        col = cols_ref[(b * ND + dist) * NS + s + k]
                        if k > 0:
                            col = jnp.where(s + k < count, col, NB)
                        acc_ref[col] += product[:, k * BS : (k + 1) * BS]

    for c in range(NB):
        out_ref[c] = acc_ref[c].astype(jnp.bfloat16)


def backward_call(sel, cols, counts, tiles, own, got, extra, along):
    added, passed = extra is not None, along is not None
    made = jax.ShapeDtypeStruct((NB, F, BS), jnp.bfloat16)
    hbm_along = [HBM] if passed else []
    return pl.pallas_call(
        functools.partial(backward_body, added, passed),
        out_shape=(made,) + ((jax.ShapeDtypeStruct(along.shape, along.dtype),) if passed else ()),
        in_specs=[SMEM] * 3 + [HBM, WHOLE, WHOLE] + ([WHOLE] if added else []) + hbm_along,
        out_specs=(WHOLE,) + tuple(hbm_along),
        scratch_shapes=[pltpu.VMEM((NB + 1, F, BS), jnp.float32)] + tile_scratch(),
        input_output_aliases={6 + added: 1} if passed else {},
        compiler_params=params(),
        cost_estimate=tile_cost(),
        name="backward_tiles",
    )(sel, cols, counts, tiles, own, got, *([extra] if added else []), *([along] if passed else []))


def final_body(kept_ref, got_ref, term_ref, out_ref):
    for c in range(2):
        spread = kept_ref[c] + got_ref[c].astype(jnp.float32)
        rows = slice(c * BS, (c + 1) * BS)
        out_ref[rows, :] = (term_ref[rows, :] + spread.T).astype(jnp.bfloat16)


def final_call(kept, got, term):
    return pl.pallas_call(
        final_body,
        out_shape=jax.ShapeDtypeStruct((256, F), jnp.bfloat16),
        compiler_params=params(),
        name="final_rows",
    )(kept, got, term)


def pick(pair, index):
    return lax.dynamic_index_in_dim(pair, index, 0, keepdims=False)


def summed_over(value, flips):
    value = value.astype(jnp.bfloat16)
    got = [send(value, flip_pairs(**f)).astype(jnp.float32) for f in flips]
    value = value.astype(jnp.float32)
    if len(got) == 1:
        return value + got[0]
    return (value + got[0]) + (got[1] + got[2])


def weight_grads(grads, sums, zh, core, nodes):
    halves = grads.reshape(2, F // 2, F)
    mine = pick(halves, core) + send(pick(halves, 1 - core), flip_pairs(dcore=1))
    bias = sums + send(sums, flip_pairs(dcore=1))
    high = bias.astype(jnp.bfloat16).astype(jnp.float32)
    pad = jnp.zeros((14, F), jnp.float32)
    value = jnp.concatenate([mine, high, bias - high, pad], 0)

    def split_bias(v):
        total = v[F // 2 : F // 2 + 1] + v[F // 2 + 1 : F // 2 + 2]
        hi = total.astype(jnp.bfloat16).astype(jnp.float32)
        return jnp.concatenate([v[: F // 2], hi, total - hi, pad], 0)

    value = split_bias(summed_over(value, [dict(dy=1), dict(dy=2), dict(dy=3)]))
    value = split_bias(summed_over(value, [dict(dx=1), dict(dx=2), dict(dx=3)]))
    value = summed_over(value, [dict(dzl=1)])
    bias = value[F // 2] + value[F // 2 + 1]
    half = value[: F // 2]
    other = send(half, flip_pairs(dzh=1))
    both = jnp.where(zh == 0, jnp.stack([half, other]), jnp.stack([other, half]))
    across = send(both, flip_pairs(dcore=1))
    low, top = jnp.where(core == 0, both, across), jnp.where(core == 0, across, both)
    norm = 1.0 / jnp.sqrt(jnp.float32(nodes))
    whole = jnp.concatenate([low, top], 1) * norm
    return whole[0], whole[1], bias * norm


def shards(
    features, tiles, tile_cols, counts, degree, train_mask, cotangent, w_self, w_neigh, bias_term
):
    rows = features.shape[0]
    rep = lax.axis_index("rep").astype(jnp.int32)
    zh, core = rep // 2, rep % 2
    place = (lax.axis_index("blk") % 8).astype(jnp.int32)
    cols = tile_cols.reshape(-1)
    live = counts.reshape(-1)

    def distance_of(k):
        return (place - (place ^ k)) % 8

    inv = 1.0 / degree.astype(jnp.float32)
    inv_col = inv.reshape(rows, 1)
    inv_row = inv.reshape(4, 1, 256)
    mask = train_mask.astype(jnp.float32).reshape(rows, 1)
    bias = bias_term.reshape(1, F)

    blocks = {}
    total = None
    for k, via in PLAN:
        source = features if via is None else blocks[k ^ via]
        blocks[k] = send(source, column_pairs(k, via))
    for k, _ in PLAN:
        total = forward_call(distance_of(k)[None], cols, live, tiles, blocks[k], total)

    parts = total.reshape(2, 2, 256, F)
    away = lax.dynamic_index_in_dim(parts, 1 - core, 1, keepdims=False).astype(jnp.bfloat16)
    kept = lax.dynamic_index_in_dim(parts, core, 1, keepdims=False)
    chip = (kept + send(away, flip_pairs(dcore=1)).astype(jnp.float32)).astype(jnp.bfloat16)
    other = send(chip, flip_pairs(dzh=1))

    activation, own_term, back_own, grads, sums = dense_call(
        rep[None], chip, other, features, cotangent, mask, inv_col, inv_row, w_self, w_neigh, bias
    )
    back_got = send(back_own, flip_pairs(dcore=1))

    extra = {}
    arrived = None
    for step, (k, via) in enumerate(reversed(PLAN)):
        sel = jnp.stack([distance_of(k), core])
        made = backward_call(
            sel, cols, live, tiles, back_own, back_got, extra.get(k), grads if step == 3 else None
        )
        if step == 3:
            grads = made[1]
        moved = send(made[0], back(column_pairs(k, via)))
        if via is None:
            moved = moved.astype(jnp.float32)
            arrived = moved if arrived is None else arrived + moved
        else:
            extra[k ^ via] = moved
    grad_self, grad_neigh, grad_bias = weight_grads(
        grads, sums, zh, core, rows * lax.axis_size("blk")
    )

    parts = arrived.reshape(2, 2, 2, F, BS)
    away = lax.dynamic_index_in_dim(parts, 1 - core, 1, keepdims=False).astype(jnp.bfloat16)
    kept = lax.dynamic_index_in_dim(parts, core, 1, keepdims=False)
    chip = kept + send(away, flip_pairs(dcore=1)).astype(jnp.float32)
    got = send(pick(chip, 1 - zh).astype(jnp.bfloat16), flip_pairs(dzh=1))
    grad_features = final_call(pick(chip, zh), got, own_term)
    return (activation, grad_features, grad_self, grad_neigh, grad_bias)


def solution(mesh):
    return jax.shard_map(
        shards,
        mesh=mesh,
        in_specs=(
            P("blk", None),
            P("blk", "rep", None, None, None),
            P("blk", "rep", None),
            P("blk", "rep"),
            P("blk"),
            P("blk"),
            P("blk", None),
            P(),
            P(),
            P(),
        ),
        out_specs=(P(("blk", "rep"), None), P(("blk", "rep"), None), P(), P(), P()),
        check_vma=False,
    )
```

```python
import functools

import jax
import jax.numpy as jnp
from jax import lax
from jax.experimental import pallas as pl
from jax.experimental.pallas import tpu as pltpu
from jax.sharding import PartitionSpec as P

AXES = ("blk", "rep")
NB = 8
ND = 8
NS = 6
BS = 128
F = 256
VMEM = 53 * 1024 * 1024
BACK_PLAN = (
    (5, 6), (4, 2), (2, None), (7, None), (1, None), (0, None), (6, None), (3, None)
)


def index_of(y, x, zl, zh, core):
    return (((y % 4 * 4 + x % 4) * 2 + zl) * 2 + zh) * 2 + core


def places():
    for t in range(128):
        yield t, t >> 5, t >> 3 & 3, t >> 2 & 1, t >> 1 & 1, t & 1


def column_pairs(k, via):
    out = []
    for t, y, x, zl, zh, core in places():
        j, r = x * 2 + zl, 2 * zh + core
        jj = j ^ k
        if via is None:
            out.append((index_of(y - r - (jj > j), jj >> 1, jj & 1, zh ^ (k & 1), core), t))
        else:
            jn = j ^ via
            out.append((index_of(y - (jj > j) + (jj > jn), jn >> 1, jn & 1, zh, core), t))
    return out


def flip_pairs(dy=0, dx=0, dzl=0, dzh=0, dcore=0):
    return [
        (t, index_of(y ^ dy, x ^ dx, zl ^ dzl, zh ^ dzh, core ^ dcore))
        for t, y, x, zl, zh, core in places()
    ]


def send(value, pairs):
    return lax.ppermute(value, AXES, pairs)


def back(pairs):
    return [(b, a) for a, b in pairs]


def params():
    return pltpu.CompilerParams(vmem_limit_bytes=VMEM)


def load_tiles(tiles_ref, dist, held_ref, sems):
    copies = [
        pltpu.make_async_copy(tiles_ref.at[b, dist], held_ref.at[b], sems.at[b]) for b in range(NB)
    ]
    for copy in copies:
        copy.start()
    return copies


def tile_scratch():
    return [pltpu.VMEM((NB, NS, BS, BS), jnp.bfloat16), pltpu.SemaphoreType.DMA((NB,))]


def tile_cost(times=1):
    return pl.CostEstimate(
        flops=2 * NB * NS * BS * BS * F * times, bytes_accessed=(8 << 20) * times, transcendentals=0
    )


SMEM = pl.BlockSpec(memory_space=pltpu.SMEM)
HBM = pl.BlockSpec(memory_space=pltpu.HBM)
WHOLE = pl.BlockSpec(memory_space=pltpu.VMEM)


def forward_body(first, passed, sel_ref, cols_ref, counts_ref, tiles_ref, shard_ref, *rest):
    held_ref, sems = rest[-2:]
    out_ref = rest[(not first) + passed]
    dist = sel_ref[0]
    copies = load_tiles(tiles_ref, dist, held_ref, sems)
    for b in range(NB):
        copies[b].wait()
        count = counts_ref[b * ND + dist]
        rows = slice(b * BS, (b + 1) * BS)
        left, right = [], []
        for s in range(NS):
            col = cols_ref[(b * ND + dist) * NS + s]
            block = shard_ref[pl.ds(pl.multiple_of(col * BS, BS), BS), :]
            right.append(jnp.where(s < count, block, jnp.zeros((), block.dtype)))
            left.append(held_ref[b, s])
        summed = jnp.dot(
            jnp.concatenate(left, 1), jnp.concatenate(right, 0), preferred_element_type=jnp.float32
        )
        out_ref[rows, :] = summed if first else rest[0][rows, :] + summed


def forward_call(dist, cols, counts, tiles, shard, total, along=None):
    first, passed = total is None, along is not None
    made = jax.ShapeDtypeStruct((NB * BS, F), jnp.float32)
    hbm_along = [HBM] if passed else []
    return pl.pallas_call(
        functools.partial(forward_body, first, passed),
        out_shape=(made,) + ((jax.ShapeDtypeStruct(along.shape, along.dtype),) if passed else ()),
        in_specs=[SMEM] * 3 + [HBM, WHOLE] + ([] if first else [WHOLE]) + hbm_along,
        out_specs=(WHOLE,) + tuple(hbm_along),
        scratch_shapes=tile_scratch(),
        input_output_aliases={5 + (not first): 1} if passed else {},
        compiler_params=params(),
        cost_estimate=tile_cost(),
        name="forward_tiles",
    )(dist, cols, counts, tiles, shard, *([] if first else [total]), *([along] if passed else []))


def dense_body(
    rep_ref, own_ref, got_ref, feat_ref, cot_ref, mask_ref, inv_ref, invt_ref, ws_ref, wn_ref,
    bias_ref, act_ref, term_ref, back_ref, grad_ref, sums_ref,
):
    rep = rep_ref[0]
    zh, core = rep // 2, rep % 2
    nt = (((1,), (1,)), ((), ()))
    tn = (((0,), (0,)), ((), ()))
    grads = jnp.zeros((F, F), jnp.float32)
    sums = jnp.zeros((1, F), jnp.float32)
    for part in range(2):
        quarter = part * 2 + core
        rows = pl.ds(pl.multiple_of(quarter * 256, 256), 256)
        feat = feat_ref[rows, :]
        summed = own_ref[part].astype(jnp.float32) + got_ref[part].astype(jnp.float32)
        agg = (summed * inv_ref[rows, :]).astype(jnp.bfloat16)
        pre = (
            jnp.dot(feat, ws_ref[...], preferred_element_type=jnp.float32)
            + jnp.dot(agg, wn_ref[...], preferred_element_type=jnp.float32)
            + bias_ref[...]
        )
        sigm = jax.nn.sigmoid(pre)
        act = (pre * sigm).astype(jnp.bfloat16)
        slope = sigm * (1.0 + pre * (1.0 - sigm))
        grad_pre = (mask_ref[rows, :] * cot_ref[rows, :].astype(jnp.float32) * slope).astype(
            jnp.bfloat16
        )

        @pl.when(zh == part)
        def _():
            act_ref[...] = act
            term_ref[...] = lax.dot_general(
                grad_pre, ws_ref[...], nt, preferred_element_type=jnp.float32
            )

        back_t = lax.dot_general(wn_ref[...], grad_pre, nt, preferred_element_type=jnp.float32)
        back_ref[part] = (back_t * invt_ref[quarter]).astype(jnp.bfloat16)
        left = jnp.where(zh == 0, feat, agg)
        grads += lax.dot_general(left, grad_pre, tn, preferred_element_type=jnp.float32)
        sums += jnp.sum(grad_pre.astype(jnp.float32), axis=0, keepdims=True)
    grad_ref[...] = grads
    sums_ref[...] = sums


def dense_call(rep, own, got, feat, cot, mask, inv, inv_t, w_self, w_neigh, bias):
    vmem = pl.BlockSpec(memory_space=pltpu.VMEM)
    return pl.pallas_call(
        dense_body,
        out_shape=(
            jax.ShapeDtypeStruct((256, F), jnp.bfloat16),
            jax.ShapeDtypeStruct((256, F), jnp.float32),
            jax.ShapeDtypeStruct((2, F, 256), jnp.bfloat16),
            jax.ShapeDtypeStruct((F, F), jnp.float32),
            jax.ShapeDtypeStruct((1, F), jnp.float32),
        ),
        in_specs=[pl.BlockSpec(memory_space=pltpu.SMEM)] + [vmem] * 10,
        out_specs=(vmem,) * 5,
        compiler_params=params(),
        name="dense_rows",
    )(rep, own, got, feat, cot, mask, inv, inv_t, w_self, w_neigh, bias)


def backward_body(
    added, passed, sel_ref, cols_ref, counts_ref, tiles_ref, own_ref, got_ref, *rest
):
    acc_ref, held_ref, sems = rest[-3:]
    out_ref = rest[added + passed]
    dist, core = sel_ref[0], sel_ref[1]
    copies = load_tiles(tiles_ref, dist, held_ref, sems)
    for c in range(NB):
        if added:
            acc_ref[c] = rest[0][c].astype(jnp.float32)
        else:
            acc_ref[c] = jnp.zeros((F, BS), jnp.float32)
    for quarter in range(NB // 2):
        mine = core == quarter % 2
        message = jnp.where(mine, own_ref[quarter // 2], got_ref[quarter // 2])
        for inner in range(2):
            b = quarter * 2 + inner
            copies[b].wait()
            count = counts_ref[b * ND + dist]
            left = message[:, inner * BS : (inner + 1) * BS]
            for s in range(0, NS, 2):
                right = jnp.concatenate([held_ref[b, s], held_ref[b, s + 1]], 1)
                product = jnp.dot(left, right, preferred_element_type=jnp.float32)
                for k in range(2):
                    col = cols_ref[(b * ND + dist) * NS + s + k]
                    col = jnp.where(s + k < count, col, NB)
                    acc_ref[col] += product[:, k * BS : (k + 1) * BS]

    for c in range(NB):
        out_ref[c] = acc_ref[c].astype(jnp.bfloat16)


def backward_call(sel, cols, counts, tiles, own, got, extra, along):
    added, passed = extra is not None, along is not None
    made = jax.ShapeDtypeStruct((NB, F, BS), jnp.bfloat16)
    hbm_along = [HBM] if passed else []
    return pl.pallas_call(
        functools.partial(backward_body, added, passed),
        out_shape=(made,) + ((jax.ShapeDtypeStruct(along.shape, along.dtype),) if passed else ()),
        in_specs=[SMEM] * 3 + [HBM, WHOLE, WHOLE] + ([WHOLE] if added else []) + hbm_along,
        out_specs=(WHOLE,) + tuple(hbm_along),
        scratch_shapes=[pltpu.VMEM((NB + 1, F, BS), jnp.float32)] + tile_scratch(),
        input_output_aliases={6 + added: 1} if passed else {},
        compiler_params=params(),
        cost_estimate=tile_cost(8),
        name="backward_tiles",
    )(sel, cols, counts, tiles, own, got, *([extra] if added else []), *([along] if passed else []))


def final_body(kept_ref, got_ref, term_ref, out_ref):
    for c in range(2):
        spread = kept_ref[c] + got_ref[c].astype(jnp.float32)
        rows = slice(c * BS, (c + 1) * BS)
        out_ref[rows, :] = (term_ref[rows, :] + spread.T).astype(jnp.bfloat16)


def final_call(kept, got, term):
    return pl.pallas_call(
        final_body,
        out_shape=jax.ShapeDtypeStruct((256, F), jnp.bfloat16),
        compiler_params=params(),
        name="final_rows",
    )(kept, got, term)


def pick(pair, index):
    return lax.dynamic_index_in_dim(pair, index, 0, keepdims=False)


def summed_over(value, flips):
    value = value.astype(jnp.bfloat16)
    got = [send(value, flip_pairs(**f)).astype(jnp.float32) for f in flips]
    value = value.astype(jnp.float32)
    if len(got) == 1:
        return value + got[0]
    return (value + got[0]) + (got[1] + got[2])


def weight_grads(grads, sums, zh, core, nodes):
    halves = grads.reshape(2, F // 2, F)
    mine = pick(halves, core) + send(pick(halves, 1 - core), flip_pairs(dcore=1))
    bias = sums + send(sums, flip_pairs(dcore=1))
    high = bias.astype(jnp.bfloat16).astype(jnp.float32)
    pad = jnp.zeros((14, F), jnp.float32)
    value = jnp.concatenate([mine, high, bias - high, pad], 0)

    def split_bias(v):
        total = v[F // 2 : F // 2 + 1] + v[F // 2 + 1 : F // 2 + 2]
        hi = total.astype(jnp.bfloat16).astype(jnp.float32)
        return jnp.concatenate([v[: F // 2], hi, total - hi, pad], 0)

    value = split_bias(summed_over(value, [dict(dy=1), dict(dy=2), dict(dy=3)]))
    value = split_bias(summed_over(value, [dict(dx=1), dict(dx=2), dict(dx=3)]))
    value = summed_over(value, [dict(dzl=1)])
    bias = value[F // 2] + value[F // 2 + 1]
    half = value[: F // 2]
    other = send(half, flip_pairs(dzh=1))
    both = jnp.where(zh == 0, jnp.stack([half, other]), jnp.stack([other, half]))
    across = send(both, flip_pairs(dcore=1))
    low, top = jnp.where(core == 0, both, across), jnp.where(core == 0, across, both)
    norm = 1.0 / jnp.sqrt(jnp.float32(nodes))
    whole = jnp.concatenate([low, top], 1) * norm
    return whole[0], whole[1], bias * norm


def shards(
    features, tiles, tile_cols, counts, degree, train_mask, cotangent, w_self, w_neigh, bias_term
):
    rows = features.shape[0]
    rep = lax.axis_index("rep").astype(jnp.int32)
    zh, core = rep // 2, rep % 2
    place = (lax.axis_index("blk") % 8).astype(jnp.int32)
    cols = tile_cols.reshape(-1)
    live = counts.reshape(-1)

    def distance_of(k):
        return (place - (place ^ k)) % 8

    inv = 1.0 / degree.astype(jnp.float32)
    inv_col = inv.reshape(rows, 1)
    inv_row = inv.reshape(4, 1, 256)
    mask = train_mask.astype(jnp.float32).reshape(rows, 1)
    bias = bias_term.reshape(1, F)

    blocks = {}
    total = None

    def fetch(k, via):
        blocks[k] = send(features if via is None else blocks[k ^ via], column_pairs(k, via))

    def consume(k, along=None):
        nonlocal total
        made = forward_call(
            distance_of(k)[None], cols, live, tiles, blocks[k], total, blocks.get(along)
        )
        total = made[0]
        if along is not None:
            blocks[along] = made[1]

    for k in (2, 6, 3, 7, 1, 0):
        fetch(k, None)
    consume(2, along=6)
    fetch(4, 2)
    consume(6, along=3)
    fetch(5, 6)
    for k in (3, 7, 1, 0, 4, 5):
        consume(k)

    parts = total.reshape(2, 2, 256, F)
    away = lax.dynamic_index_in_dim(parts, 1 - core, 1, keepdims=False).astype(jnp.bfloat16)
    kept = lax.dynamic_index_in_dim(parts, core, 1, keepdims=False)
    chip = (kept + send(away, flip_pairs(dcore=1)).astype(jnp.float32)).astype(jnp.bfloat16)
    other = send(chip, flip_pairs(dzh=1))

    activation, own_term, back_own, grads, sums = dense_call(
        rep[None], chip, other, features, cotangent, mask, inv_col, inv_row, w_self, w_neigh, bias
    )
    back_got = send(back_own, flip_pairs(dcore=1))

    extra = {}
    arrived = None
    for k, via in BACK_PLAN:
        sel = jnp.stack([distance_of(k), core])
        along = grads if k == 5 else None
        made = backward_call(sel, cols, live, tiles, back_own, back_got, extra.get(k), along)
        if along is not None:
            grads = made[1]
        moved = send(made[0], back(column_pairs(k, via)))
        if via is None:
            moved = moved.astype(jnp.float32)
            arrived = moved if arrived is None else arrived + moved
        else:
            extra[k ^ via] = moved
    grad_self, grad_neigh, grad_bias = weight_grads(
        grads, sums, zh, core, rows * lax.axis_size("blk")
    )

    parts = arrived.reshape(2, 2, 2, F, BS)
    away = lax.dynamic_index_in_dim(parts, 1 - core, 1, keepdims=False).astype(jnp.bfloat16)
    kept = lax.dynamic_index_in_dim(parts, core, 1, keepdims=False)
    chip = kept + send(away, flip_pairs(dcore=1)).astype(jnp.float32)
    got = send(pick(chip, 1 - zh).astype(jnp.bfloat16), flip_pairs(dzh=1))
    grad_features = final_call(pick(chip, zh), got, own_term)
    return (activation, grad_features, grad_self, grad_neigh, grad_bias)


def solution(mesh):
    return jax.shard_map(
        shards,
        mesh=mesh,
        in_specs=(
            P("blk", None),
            P("blk", "rep", None, None, None),
            P("blk", "rep", None),
            P("blk", "rep"),
            P("blk"),
            P("blk"),
            P("blk", None),
            P(),
            P(),
            P(),
        ),
        out_specs=(P(("blk", "rep"), None), P(("blk", "rep"), None), P(), P(), P()),
        check_vma=False,
    )
```

```python
import functools

import jax
import jax.numpy as jnp
from jax import lax
from jax.experimental import pallas as pl
from jax.experimental.pallas import tpu as pltpu
from jax.sharding import PartitionSpec as P

AXES = ("blk", "rep")
NB = 8
ND = 8
NS = 6
BS = 128
F = 256
VMEM = 53 * 1024 * 1024
PLAN = {6: None, 2: None, 1: None, 4: 2, 7: None, 3: None, 0: None, 5: 1}
CROSS = {1: 0x7776, 3: 0xDFFF, 7: 0xDFEF}
GROUPS = ((6, 2, 1), (4, 7, 3), (0,), (5,))
BACK = ((5, ()), (2, (5,)), (1, (2,)), (4, (1,)), (7, (4,)), (3, (7,)), (0, (3,)), (6, (0,)))


def index_of(y, x, zl, zh, core):
    return (((y % 4 * 4 + x % 4) * 2 + zl) * 2 + zh) * 2 + core


def places():
    for t in range(128):
        yield t, t >> 5, t >> 3 & 3, t >> 2 & 1, t >> 1 & 1, t & 1


def column_pairs(k):
    via = PLAN[k]
    out = []
    for t, y, x, zl, zh, core in places():
        j, r = x * 2 + zl, 2 * zh + core
        jj = j ^ k
        if via is None:
            flip = CROSS[k] >> (jj * 2 + core) & 1 if k & 1 else 0
            out.append((index_of(y - r - (jj > j), jj >> 1, jj & 1, zh ^ flip, core), t))
        else:
            jn = j ^ via
            out.append((index_of(y - (jj > j) + (jj > jn), jn >> 1, jn & 1, zh, core), t))
    return out


def flip_pairs(dy=0, dx=0, dzl=0, dzh=0, dcore=0):
    return [
        (t, index_of(y ^ dy, x ^ dx, zl ^ dzl, zh ^ dzh, core ^ dcore))
        for t, y, x, zl, zh, core in places()
    ]


def send(value, pairs):
    return lax.ppermute(value, AXES, pairs)


def params(limit=VMEM):
    return pltpu.CompilerParams(vmem_limit_bytes=limit)


SMEM = pl.BlockSpec(memory_space=pltpu.SMEM)
HBM = pl.BlockSpec(memory_space=pltpu.HBM)
UNREAD = pl.BlockSpec(memory_space=pl.ANY)
WHOLE = pl.BlockSpec(memory_space=pltpu.VMEM)


def tile_cost(n):
    return pl.CostEstimate(
        flops=2 * NB * NS * BS * BS * F * n, bytes_accessed=(8 << 20) * n, transcendentals=0
    )


def forward_body(n, first, last, sel_ref, cols_ref, counts_ref, tiles_ref, *rest):
    shards = rest[:n]
    before = None if first else rest[n]
    outs = rest[n + (not first) : -3]
    total_ref, held_ref, sems = rest[-3:]
    i, half = pl.program_id(0), pl.program_id(1)
    dist = sel_ref[i]

    def fetch(k):
        return pltpu.make_async_copy(shards[k], held_ref.at[k % 2], sems.at[k % 2])

    @pl.when((i == 0) & (half == 0))
    def _():
        fetch(0).start()

    for k in range(n):

        @pl.when((i == k) & (half == 0))
        def _():
            fetch(k).wait()
            if k + 1 < n:
                fetch(k + 1).start()

    def block_row(inner, carry):
        b = half * 4 + inner
        count = counts_ref[b * ND + dist]
        left, right = [], []
        for s in range(NS):
            col = cols_ref[(b * ND + dist) * NS + s]
            block = held_ref[i % 2, pl.ds(pl.multiple_of(col * BS, BS), BS), :]
            right.append(jnp.where(s < count, block, jnp.zeros((), block.dtype)))
            left.append(tiles_ref[inner, 0, s])
        summed = jnp.dot(
            jnp.concatenate(left, 1), jnp.concatenate(right, 0), preferred_element_type=jnp.float32
        )
        rows = pl.ds(pl.multiple_of(b * BS, BS), BS)

        @pl.when(i == 0)
        def _():
            total_ref[rows, :] = summed if first else before[rows, :] + summed

        @pl.when(i > 0)
        def _():
            total_ref[rows, :] += summed

        return carry

    lax.fori_loop(0, 4, block_row, 0, unroll=2)

    @pl.when((i == n - 1) & (half == 1))
    def _():
        if last:
            core = sel_ref[n]
            for part in range(2):
                keep = pl.multiple_of((part * 2 + core) * 256, 256)
                away = pl.multiple_of((part * 2 + 1 - core) * 256, 256)
                outs[0][part] = total_ref[pl.ds(keep, 256), :]
                outs[1][part] = total_ref[pl.ds(away, 256), :].astype(jnp.bfloat16)
        else:
            outs[0][...] = total_ref[...]


def forward_call(sel, cols, counts, tiles, shards, before, last):
    n, first = len(shards), before is None

    def full(shape):
        return pl.BlockSpec(shape, lambda *_: (0,) * len(shape))

    if last:
        out_shape = (
            jax.ShapeDtypeStruct((2, 256, F), jnp.float32),
            jax.ShapeDtypeStruct((2, 256, F), jnp.bfloat16),
        )
    else:
        out_shape = (jax.ShapeDtypeStruct((NB * BS, F), jnp.float32),)
    tile_spec = pl.BlockSpec((4, 1, NS, BS, BS), lambda i, h, sel, c, m: (h, sel[i], 0, 0, 0))
    return pl.pallas_call(
        functools.partial(forward_body, n, first, last),
        out_shape=out_shape,
        grid_spec=pltpu.PrefetchScalarGridSpec(
            num_scalar_prefetch=3,
            grid=(n, 2),
            in_specs=[tile_spec] + [HBM] * n + ([] if first else [full((NB * BS, F))]),
            out_specs=tuple(full(o.shape) for o in out_shape),
            scratch_shapes=[
                pltpu.VMEM((NB * BS, F), jnp.float32),
                pltpu.VMEM((2, NB * BS, F), jnp.bfloat16),
                pltpu.SemaphoreType.DMA((2,)),
            ],
        ),
        compiler_params=params(),
        cost_estimate=tile_cost(n),
        name="forward_tiles",
    )(sel, cols, counts, tiles, *shards, *([] if first else [before]))


def dense_body(
    rep_ref, own_ref, got_ref, feat_ref, cot_ref, mask_ref, inv_ref, invt_ref, ws_ref, wn_ref,
    bias_ref, act_ref, term_ref, back_ref, grad_ref, sums_ref,
):
    rep = rep_ref[0]
    zh, core = rep // 2, rep % 2
    nt = (((1,), (1,)), ((), ()))
    tn = (((0,), (0,)), ((), ()))
    grads = jnp.zeros((F, F), jnp.float32)
    sums = jnp.zeros((1, F), jnp.float32)
    for part in range(2):
        quarter = part * 2 + core
        rows = pl.ds(pl.multiple_of(quarter * 256, 256), 256)
        feat = feat_ref[rows, :]
        summed = own_ref[part].astype(jnp.float32) + got_ref[part].astype(jnp.float32)
        agg = (summed * inv_ref[rows, :]).astype(jnp.bfloat16)
        pre = (
            jnp.dot(feat, ws_ref[...], preferred_element_type=jnp.float32)
            + jnp.dot(agg, wn_ref[...], preferred_element_type=jnp.float32)
            + bias_ref[...]
        )
        sigm = jax.nn.sigmoid(pre)
        act = (pre * sigm).astype(jnp.bfloat16)
        slope = sigm * (1.0 + pre * (1.0 - sigm))
        grad_pre = (mask_ref[rows, :] * cot_ref[rows, :].astype(jnp.float32) * slope).astype(
            jnp.bfloat16
        )

        @pl.when(zh == part)
        def _():
            act_ref[...] = act
            term_ref[...] = lax.dot_general(
                grad_pre, ws_ref[...], nt, preferred_element_type=jnp.float32
            )

        back_t = lax.dot_general(wn_ref[...], grad_pre, nt, preferred_element_type=jnp.float32)
        back_ref[part] = (back_t * invt_ref[quarter]).astype(jnp.bfloat16)
        left = jnp.where(zh == 0, feat, agg)
        grads += lax.dot_general(left, grad_pre, tn, preferred_element_type=jnp.float32)
        sums += jnp.sum(grad_pre.astype(jnp.float32), axis=0, keepdims=True)
    grad_ref[...] = grads
    sums_ref[...] = sums


def dense_call(rep, own, got, feat, cot, mask, inv, inv_t, w_self, w_neigh, bias):
    vmem = pl.BlockSpec(memory_space=pltpu.VMEM)
    return pl.pallas_call(
        dense_body,
        out_shape=(
            jax.ShapeDtypeStruct((256, F), jnp.bfloat16),
            jax.ShapeDtypeStruct((256, F), jnp.float32),
            jax.ShapeDtypeStruct((2, F, 256), jnp.bfloat16),
            jax.ShapeDtypeStruct((F, F), jnp.float32),
            jax.ShapeDtypeStruct((1, F), jnp.float32),
        ),
        in_specs=[pl.BlockSpec(memory_space=pltpu.SMEM)] + [vmem] * 10,
        out_specs=(vmem,) * 5,
        compiler_params=params(16 << 20),
        name="dense_rows",
    )(rep, own, got, feat, cot, mask, inv, inv_t, w_self, w_neigh, bias)


def backward_body(added, sel_ref, cols_ref, counts_ref, tiles_ref, own_ref, got_ref, *rest):
    out_ref, acc_ref = rest[-2:]
    step = pl.program_id(0)
    dist, core = sel_ref[0], sel_ref[1]

    @pl.when(step == 0)
    def _():
        for c in range(NB):
            if added:
                acc_ref[c] = rest[0][c].astype(jnp.float32)
            else:
                acc_ref[c] = jnp.zeros((F, BS), jnp.float32)

    message = jnp.where(step % 2 == core, own_ref[step // 2], got_ref[step // 2])
    for inner in range(2):
        b = step * 2 + inner
        count = counts_ref[b * ND + dist]
        left = message[:, inner * BS : (inner + 1) * BS]
        for s in range(0, NS, 2):
            right = jnp.concatenate([tiles_ref[inner, 0, s], tiles_ref[inner, 0, s + 1]], 1)
            product = jnp.dot(left, right, preferred_element_type=jnp.float32)
            for k in range(2):
                col = cols_ref[(b * ND + dist) * NS + s + k]
                col = jnp.where(s + k < count, col, NB)
                acc_ref[col] += product[:, k * BS : (k + 1) * BS]

    @pl.when(step == NB // 2 - 1)
    def _():
        for c in range(NB):
            out_ref[c] = acc_ref[c].astype(jnp.bfloat16)


def backward_call(sel, cols, counts, tiles, own, got, extra, after):
    added = extra is not None
    whole = pl.BlockSpec((NB, F, BS), lambda i, *_: (0, 0, 0))
    message = pl.BlockSpec((2, F, 256), lambda i, *_: (0, 0, 0))
    tile_spec = pl.BlockSpec((2, 1, NS, BS, BS), lambda i, sel, c, n: (i, sel[0], 0, 0, 0))
    return pl.pallas_call(
        functools.partial(backward_body, added),
        out_shape=jax.ShapeDtypeStruct((NB, F, BS), jnp.bfloat16),
        grid_spec=pltpu.PrefetchScalarGridSpec(
            num_scalar_prefetch=3,
            grid=(NB // 2,),
            in_specs=[tile_spec, message, message]
            + ([whole] if added else [])
            + [UNREAD] * len(after),
            out_specs=whole,
            scratch_shapes=[pltpu.VMEM((NB + 1, F, BS), jnp.float32)],
        ),
        compiler_params=params(),
        cost_estimate=tile_cost(1),
        name="backward_tiles",
    )(sel, cols, counts, tiles, own, got, *([extra] if added else []), *after)


def split_body(core_ref, along_ref, *rest):
    arrived, (_, keep_ref, away_ref) = rest[:-3], rest[-3:]
    core = core_ref[0]
    for part in range(2):
        for c in range(2):
            keep = (part * 2 + core) * 2 + c
            away = (part * 2 + 1 - core) * 2 + c
            kept = arrived[0][keep].astype(jnp.float32)
            sent = arrived[0][away].astype(jnp.float32)
            for ref in arrived[1:]:
                kept += ref[keep].astype(jnp.float32)
                sent += ref[away].astype(jnp.float32)
            keep_ref[part, c] = kept
            away_ref[part, c] = sent.astype(jnp.bfloat16)


def split_call(core, arrived, along):
    return pl.pallas_call(
        split_body,
        out_shape=(
            jax.ShapeDtypeStruct(along.shape, along.dtype),
            jax.ShapeDtypeStruct((2, 2, F, BS), jnp.float32),
            jax.ShapeDtypeStruct((2, 2, F, BS), jnp.bfloat16),
        ),
        in_specs=[SMEM, UNREAD] + [WHOLE] * len(arrived),
        out_specs=(UNREAD, WHOLE, WHOLE),
        input_output_aliases={1: 0},
        compiler_params=params(16 << 20),
        name="split_products",
    )(core, along, *arrived)


def final_body(kept_ref, got_ref, term_ref, out_ref):
    for c in range(2):
        spread = kept_ref[c] + got_ref[c].astype(jnp.float32)
        rows = slice(c * BS, (c + 1) * BS)
        out_ref[rows, :] = (term_ref[rows, :] + spread.T).astype(jnp.bfloat16)


def final_call(kept, got, term):
    return pl.pallas_call(
        final_body,
        out_shape=jax.ShapeDtypeStruct((256, F), jnp.bfloat16),
        compiler_params=params(16 << 20),
        name="final_rows",
    )(kept, got, term)


def pick(pair, index):
    return lax.dynamic_index_in_dim(pair, index, 0, keepdims=False)


def summed_over(value, flips):
    value = value.astype(jnp.bfloat16)
    got = [send(value, flip_pairs(**f)).astype(jnp.float32) for f in flips]
    value = value.astype(jnp.float32)
    if len(got) == 1:
        return value + got[0]
    return (value + got[0]) + (got[1] + got[2])


def weight_grads(grads, sums, zh, core, nodes):
    halves = grads.reshape(2, F // 2, F)
    mine = pick(halves, core) + send(pick(halves, 1 - core), flip_pairs(dcore=1))
    bias = sums + send(sums, flip_pairs(dcore=1))
    high = bias.astype(jnp.bfloat16).astype(jnp.float32)
    pad = jnp.zeros((14, F), jnp.float32)
    value = jnp.concatenate([mine, high, bias - high, pad], 0)

    def split_bias(v):
        total = v[F // 2 : F // 2 + 1] + v[F // 2 + 1 : F // 2 + 2]
        hi = total.astype(jnp.bfloat16).astype(jnp.float32)
        return jnp.concatenate([v[: F // 2], hi, total - hi, pad], 0)

    value = split_bias(summed_over(value, [dict(dy=1), dict(dy=2), dict(dy=3)]))
    value = split_bias(summed_over(value, [dict(dx=1), dict(dx=2), dict(dx=3)]))
    value = summed_over(value, [dict(dzl=1)])
    bias = value[F // 2] + value[F // 2 + 1]
    half = value[: F // 2]
    other = send(half, flip_pairs(dzh=1))
    both = jnp.where(zh == 0, jnp.stack([half, other]), jnp.stack([other, half]))
    across = send(both, flip_pairs(dcore=1))
    low, top = jnp.where(core == 0, both, across), jnp.where(core == 0, across, both)
    norm = 1.0 / jnp.sqrt(jnp.float32(nodes))
    whole = jnp.concatenate([low, top], 1) * norm
    return whole[0], whole[1], bias * norm


def shards(
    features, tiles, tile_cols, counts, degree, train_mask, cotangent, w_self, w_neigh, bias_term
):
    rows = features.shape[0]
    rep = lax.axis_index("rep").astype(jnp.int32)
    zh, core = rep // 2, rep % 2
    place = (lax.axis_index("blk") % 8).astype(jnp.int32)
    cols = tile_cols.reshape(-1)
    live = counts.reshape(-1)

    def distance_of(k):
        return (place - (place ^ k)) % 8

    inv = 1.0 / degree.astype(jnp.float32)
    inv_col = inv.reshape(rows, 1)
    inv_row = inv.reshape(4, 1, 256)
    mask = train_mask.astype(jnp.float32).reshape(rows, 1)
    bias = bias_term.reshape(1, F)

    blocks = {}
    for k, via in PLAN.items():
        blocks[k] = send(features if via is None else blocks[k ^ via], column_pairs(k))
    made = (None,)
    for group in GROUPS:
        last = group is GROUPS[-1]
        sel = jnp.stack([distance_of(k) for k in group] + [core])
        shards = [blocks[k] for k in group]
        made = forward_call(sel, cols, live, tiles, shards, made[0], last)

    kept, away = made
    chip = (kept + send(away, flip_pairs(dcore=1)).astype(jnp.float32)).astype(jnp.bfloat16)
    other = send(chip, flip_pairs(dzh=1))

    activation, own_term, back_own, grads, sums = dense_call(
        rep[None], chip, other, features, cotangent, mask, inv_col, inv_row, w_self, w_neigh, bias
    )
    back_got = send(back_own, flip_pairs(dcore=1))

    arrived, extra, products = {}, {}, {}
    for k, after in BACK:
        sel = jnp.stack([distance_of(k), core])
        products[k] = backward_call(
            sel, cols, live, tiles, back_own, back_got, extra.get(k), [products[a] for a in after]
        )
        moved = send(products[k], [(b, a) for a, b in column_pairs(k)])
        if PLAN[k] is None:
            arrived[k] = moved
        else:
            extra[k ^ PLAN[k]] = moved
    grads, kept, away = split_call(core[None], list(arrived.values()), grads)
    grad_self, grad_neigh, grad_bias = weight_grads(
        grads, sums, zh, core, rows * lax.axis_size("blk")
    )

    chip = kept + send(away, flip_pairs(dcore=1)).astype(jnp.float32)
    got = send(pick(chip, 1 - zh).astype(jnp.bfloat16), flip_pairs(dzh=1))
    grad_features = final_call(pick(chip, zh), got, own_term)
    return (activation, grad_features, grad_self, grad_neigh, grad_bias)


def solution(mesh):
    return jax.shard_map(
        shards,
        mesh=mesh,
        in_specs=(
            P("blk", None),
            P("blk", "rep", None, None, None),
            P("blk", "rep", None),
            P("blk", "rep"),
            P("blk"),
            P("blk"),
            P("blk", None),
            P(),
            P(),
            P(),
        ),
        out_specs=(P(("blk", "rep"), None), P(("blk", "rep"), None), P(), P(), P()),
        check_vma=False,
    )
```

```python
import functools

import jax
import jax.numpy as jnp
from jax import lax
from jax.experimental import pallas as pl
from jax.experimental.pallas import tpu as pltpu
from jax.sharding import PartitionSpec as P

AXES = ("blk", "rep")
NB = 8
ND = 8
NS = 6
BS = 128
F = 256
VMEM = 16 * 1024 * 1024
ASSEMBLE_VMEM = 40 * 1024 * 1024
PLAN = {6: None, 3: None, 1: None, 2: None, 0: None, 7: 1, 4: 2, 5: 6}
CROSS = {1: 0x7666, 3: 0x5FDB}
GROUPS = ((6, 3, 1, 2, 0), (7, 4, 5))
HELD = ((6, (1,)), (3, (2, 0)))
BACK = ((7, ()), (4, ()), (5, ()), (2, ()), (1, ()), (0, ()), (6, (2,)), (3, (1,)))
MADE = (6, 3)
EARLY = (0,)


def index_of(y, x, zl, zh, core):
    return (((y % 4 * 4 + x % 4) * 2 + zl) * 2 + zh) * 2 + core


def places():
    for t in range(128):
        yield t, t >> 5, t >> 3 & 3, t >> 2 & 1, t >> 1 & 1, t & 1


def column_pairs(k):
    via = PLAN[k]
    out = []
    for t, y, x, zl, zh, core in places():
        j, r = x * 2 + zl, 2 * zh + core
        jj = j ^ k
        if via is None:
            flip = CROSS[k] >> (jj * 2 + core) & 1 if k & 1 else 0
            out.append((index_of(y - r - (jj > j), jj >> 1, jj & 1, zh ^ flip, core), t))
        else:
            jn = j ^ via
            out.append((index_of(y - (jj > j) + (jj > jn), jn >> 1, jn & 1, zh, core), t))
    return out


def flip_pairs(dy=0, dx=0, dzl=0, dzh=0, dcore=0):
    return [
        (t, index_of(y ^ dy, x ^ dx, zl ^ dzl, zh ^ dzh, core ^ dcore))
        for t, y, x, zl, zh, core in places()
    ]


def send(value, pairs):
    return lax.ppermute(value, AXES, pairs)


def params(limit=VMEM):
    return pltpu.CompilerParams(vmem_limit_bytes=limit)


SMEM = pl.BlockSpec(memory_space=pltpu.SMEM)
HBM = pl.BlockSpec(memory_space=pltpu.HBM)
UNREAD = pl.BlockSpec(memory_space=pl.ANY)
WHOLE = pl.BlockSpec(memory_space=pltpu.VMEM)


def matmul_cost(n):
    return pl.CostEstimate(
        flops=2 * NB * NB * BS * BS * F * n, bytes_accessed=(3 << 20) * n, transcendentals=0
    )


def assemble_body(n, sel_ref, cols_ref, counts_ref, tiles_ref, *rest):
    outs, (held_ref, sems) = rest[:n], rest[n:]

    def fetch(k):
        dist, slot = sel_ref[k], k % 2
        return pltpu.make_async_copy(tiles_ref.at[:, dist], held_ref.at[slot], sems.at[slot])

    fetch(0).start()
    for k in range(n):
        fetch(k).wait()
        if k + 1 < n:
            fetch(k + 1).start()
        dist, out_ref, slot = sel_ref[k], outs[k], k % 2

        def block_row(b, carry):
            count = counts_ref[b * ND + dist]
            rows = pl.ds(pl.multiple_of(b * BS, BS), BS)
            cols = [cols_ref[(b * ND + dist) * NS + s] for s in range(NS)]
            cols = [jnp.where(s < count, cols[s], NB) for s in range(NS)]
            tiles = [held_ref[slot, b, s] for s in range(NS)]
            zero = jnp.zeros((BS, BS), jnp.bfloat16)
            for c in range(NB):
                parts = [jnp.where(cols[s] == c, tiles[s], zero) for s in range(NS)]
                pairs = [parts[s] + parts[s + 1] for s in range(0, NS, 2)]
                out_ref[c, rows, :] = pairs[0] + pairs[1] + pairs[2]
            return carry

        lax.fori_loop(0, NB, block_row, 0)


def assemble_call(sel, cols, counts, tiles):
    n = sel.shape[0]
    return pl.pallas_call(
        functools.partial(assemble_body, n),
        out_shape=(jax.ShapeDtypeStruct((NB, NB * BS, BS), jnp.bfloat16),) * n,
        in_specs=[SMEM] * 3 + [HBM],
        out_specs=(WHOLE,) * n,
        scratch_shapes=[
            pltpu.VMEM((2, NB, NS, BS, BS), jnp.bfloat16),
            pltpu.SemaphoreType.DMA((2,)),
        ],
        compiler_params=params(ASSEMBLE_VMEM),
        cost_estimate=matmul_cost(n),
        name="assemble_adjacency",
    )(sel, cols, counts, tiles)


def wide(adj_ref):
    return jnp.concatenate([adj_ref[c] for c in range(NB)], 1)


def forward_body(n, first, last, core_ref, *refs):
    adjacency, shards, rest = refs[:n], refs[n : 2 * n], refs[2 * n :]
    outs = rest[-3:-1] if last else rest[-2:-1]
    total_ref = rest[-1]
    for k in range(n):
        product = jnp.dot(wide(adjacency[k]), shards[k][...], preferred_element_type=jnp.float32)
        if k > 0:
            total_ref[...] += product
        else:
            total_ref[...] = product if first else rest[0][...] + product
    if last:
        core = core_ref[0]
        for part in range(2):
            keep = pl.multiple_of((part * 2 + core) * 256, 256)
            away = pl.multiple_of((part * 2 + 1 - core) * 256, 256)
            outs[0][part] = total_ref[pl.ds(keep, 256), :]
            outs[1][part] = total_ref[pl.ds(away, 256), :].astype(jnp.bfloat16)
    else:
        outs[0][...] = total_ref[...]


def forward_call(core, adjacency, shards, before, last, after):
    n, first = len(shards), before is None
    if last:
        out_shape = (
            jax.ShapeDtypeStruct((2, 256, F), jnp.float32),
            jax.ShapeDtypeStruct((2, 256, F), jnp.bfloat16),
        )
    else:
        out_shape = (jax.ShapeDtypeStruct((NB * BS, F), jnp.float32),)
    return pl.pallas_call(
        functools.partial(forward_body, n, first, last),
        out_shape=out_shape,
        in_specs=[SMEM] + [WHOLE] * (2 * n + (not first)) + [UNREAD] * len(after),
        out_specs=(WHOLE,) * len(out_shape),
        scratch_shapes=[pltpu.VMEM((NB * BS, F), jnp.float32)],
        compiler_params=params(),
        cost_estimate=matmul_cost(n),
        name="forward_product",
    )(core, *adjacency, *shards, *([] if first else [before]), *after)


def dense_body(
    rep_ref, own_ref, got_ref, feat_ref, cot_ref, mask_ref, inv_ref, invt_ref, ws_ref, wn_ref,
    bias_ref, act_ref, term_ref, back_ref, grad_ref, sums_ref,
):
    rep = rep_ref[0]
    zh, core = rep // 2, rep % 2
    nt = (((1,), (1,)), ((), ()))
    tn = (((0,), (0,)), ((), ()))
    grads = jnp.zeros((F, F), jnp.float32)
    sums = jnp.zeros((1, F), jnp.float32)
    for part in range(2):
        quarter = part * 2 + core
        rows = pl.ds(pl.multiple_of(quarter * 256, 256), 256)
        feat = feat_ref[rows, :]
        summed = own_ref[part].astype(jnp.float32) + got_ref[part].astype(jnp.float32)
        agg = (summed * inv_ref[rows, :]).astype(jnp.bfloat16)
        pre = (
            jnp.dot(feat, ws_ref[...], preferred_element_type=jnp.float32)
            + jnp.dot(agg, wn_ref[...], preferred_element_type=jnp.float32)
            + bias_ref[...]
        )
        sigm = jax.nn.sigmoid(pre)
        act = (pre * sigm).astype(jnp.bfloat16)
        slope = sigm * (1.0 + pre * (1.0 - sigm))
        grad_pre = (mask_ref[rows, :] * cot_ref[rows, :].astype(jnp.float32) * slope).astype(
            jnp.bfloat16
        )

        @pl.when(zh == part)
        def _():
            act_ref[...] = act
            term_ref[...] = lax.dot_general(
                grad_pre, ws_ref[...], nt, preferred_element_type=jnp.float32
            )

        back_t = lax.dot_general(wn_ref[...], grad_pre, nt, preferred_element_type=jnp.float32)
        back_ref[part] = (back_t * invt_ref[quarter]).astype(jnp.bfloat16)
        left = jnp.where(zh == 0, feat, agg)
        grads += lax.dot_general(left, grad_pre, tn, preferred_element_type=jnp.float32)
        sums += jnp.sum(grad_pre.astype(jnp.float32), axis=0, keepdims=True)
    grad_ref[...] = grads
    sums_ref[...] = sums


def dense_call(rep, own, got, feat, cot, mask, inv, inv_t, w_self, w_neigh, bias):
    vmem = pl.BlockSpec(memory_space=pltpu.VMEM)
    return pl.pallas_call(
        dense_body,
        out_shape=(
            jax.ShapeDtypeStruct((256, F), jnp.bfloat16),
            jax.ShapeDtypeStruct((256, F), jnp.float32),
            jax.ShapeDtypeStruct((2, F, 256), jnp.bfloat16),
            jax.ShapeDtypeStruct((F, F), jnp.float32),
            jax.ShapeDtypeStruct((1, F), jnp.float32),
        ),
        in_specs=[pl.BlockSpec(memory_space=pltpu.SMEM)] + [vmem] * 10,
        out_specs=(vmem,) * 5,
        compiler_params=params(16 << 20),
        name="dense_rows",
    )(rep, own, got, feat, cot, mask, inv, inv_t, w_self, w_neigh, bias)


def backward_body(added, core_ref, adj_ref, own_ref, got_ref, *rest):
    out_ref = rest[-1]
    core = core_ref[0]
    message = []
    for quarter in range(4):
        mine = core == quarter % 2
        message.append(jnp.where(mine, own_ref[quarter // 2], got_ref[quarter // 2]))
    product = jnp.dot(
        jnp.concatenate(message, 1), wide(adj_ref), preferred_element_type=jnp.float32
    )
    for c in range(NB):
        part = product[:, c * BS : (c + 1) * BS]
        for ref in rest[:added]:
            part += ref[c].astype(jnp.float32)
        out_ref[c] = part.astype(jnp.bfloat16)


def backward_call(core, adjacency, own, got, extra, after):
    added = len(extra)
    return pl.pallas_call(
        functools.partial(backward_body, added),
        out_shape=jax.ShapeDtypeStruct((NB, F, BS), jnp.bfloat16),
        in_specs=[SMEM] + [WHOLE] * (3 + added) + [UNREAD] * len(after),
        out_specs=WHOLE,
        compiler_params=params(),
        cost_estimate=matmul_cost(1),
        name="backward_product",
    )(core, adjacency, own, got, *extra, *after)


def split_body(core_ref, *rest):
    arrived, (keep_ref, away_ref) = rest[:-2], rest[-2:]
    core = core_ref[0]
    for part in range(2):
        for c in range(2):
            keep = (part * 2 + core) * 2 + c
            away = (part * 2 + 1 - core) * 2 + c
            kept = arrived[0][keep].astype(jnp.float32)
            sent = arrived[0][away].astype(jnp.float32)
            for ref in arrived[1:]:
                kept += ref[keep].astype(jnp.float32)
                sent += ref[away].astype(jnp.float32)
            keep_ref[part, c] = kept
            away_ref[part, c] = sent.astype(jnp.bfloat16)


def split_call(core, arrived):
    return pl.pallas_call(
        split_body,
        out_shape=(
            jax.ShapeDtypeStruct((2, 2, F, BS), jnp.float32),
            jax.ShapeDtypeStruct((2, 2, F, BS), jnp.bfloat16),
        ),
        in_specs=[SMEM] + [WHOLE] * len(arrived),
        out_specs=(WHOLE, WHOLE),
        compiler_params=params(16 << 20),
        name="split_products",
    )(core, *arrived)


def hold_body(*refs):
    pass


def hold_call(along, after):
    return pl.pallas_call(
        hold_body,
        out_shape=jax.ShapeDtypeStruct(along.shape, along.dtype),
        in_specs=[UNREAD] * (1 + len(after)),
        out_specs=UNREAD,
        input_output_aliases={0: 0},
        name="hold",
    )(along, *after)


def final_body(kept_ref, got_ref, term_ref, out_ref):
    for c in range(2):
        spread = kept_ref[c] + got_ref[c].astype(jnp.float32)
        rows = slice(c * BS, (c + 1) * BS)
        out_ref[rows, :] = (term_ref[rows, :] + spread.T).astype(jnp.bfloat16)


def final_call(kept, got, term):
    return pl.pallas_call(
        final_body,
        out_shape=jax.ShapeDtypeStruct((256, F), jnp.bfloat16),
        compiler_params=params(16 << 20),
        name="final_rows",
    )(kept, got, term)


def pick(pair, index):
    return lax.dynamic_index_in_dim(pair, index, 0, keepdims=False)


def weight_grads(grads, sums, zh, core, nodes):
    halves = grads.reshape(2, F // 2, F)
    mine = pick(halves, core) + send(pick(halves, 1 - core), flip_pairs(dcore=1))
    count = lax.axis_size("blk")
    share = F // 2 // count
    bias = sums + send(sums, flip_pairs(dcore=1))
    high = bias.astype(jnp.bfloat16)
    low = (bias - high.astype(jnp.float32)).astype(jnp.bfloat16)
    bias_rows = jnp.broadcast_to(jnp.concatenate([high, low], 0)[None], (count, 2, F))
    rows = mine.astype(jnp.bfloat16).reshape(count, share, F)
    parts = lax.all_to_all(jnp.concatenate([rows, bias_rows], 1), "blk", 0, 0)
    total = jnp.sum(parts.astype(jnp.float32), axis=0)
    bias = total[share] + total[share + 1]
    spread = jnp.broadcast_to(total[None, :share], (count, share, F))
    half = lax.all_to_all(spread, "blk", 0, 0).reshape(F // 2, F)
    other = send(half, flip_pairs(dzh=1))
    both = jnp.where(zh == 0, jnp.stack([half, other]), jnp.stack([other, half]))
    across = send(both, flip_pairs(dcore=1))
    low, top = jnp.where(core == 0, both, across), jnp.where(core == 0, across, both)
    norm = 1.0 / jnp.sqrt(jnp.float32(nodes))
    whole = jnp.concatenate([low, top], 1) * norm
    return whole[0], whole[1], bias * norm


def shards(
    features, tiles, tile_cols, counts, degree, train_mask, cotangent, w_self, w_neigh, bias_term
):
    rows = features.shape[0]
    rep = lax.axis_index("rep").astype(jnp.int32)
    zh, core = rep // 2, rep % 2
    place = (lax.axis_index("blk") % 8).astype(jnp.int32)
    cols = tile_cols.reshape(-1)
    live = counts.reshape(-1)

    def distance_of(k):
        return (place - (place ^ k)) % 8

    inv = 1.0 / degree.astype(jnp.float32)
    inv_col = inv.reshape(rows, 1)
    inv_row = inv.reshape(4, 1, 256)
    mask = train_mask.astype(jnp.float32).reshape(rows, 1)
    bias = bias_term.reshape(1, F)

    order = list(PLAN)
    sel = jnp.stack([distance_of(k) for k in order])
    adjacency = dict(zip(order, assemble_call(sel, cols, live, tiles)))
    blocks, held = {}, []
    for k, via in PLAN.items():
        if via is None:
            blocks[k] = send(features, column_pairs(k))
    for k, after in HELD:
        blocks[k] = hold_call(blocks[k], [adjacency[k]] + [blocks[a] for a in after])
        held.append(blocks[k])
    for k, via in PLAN.items():
        if via is not None:
            blocks[k] = send(blocks[k ^ via], column_pairs(k))
    made = (None,)
    for group in GROUPS:
        made = forward_call(
            core[None],
            [adjacency[k] for k in group],
            [blocks[k] for k in group],
            made[0],
            group is GROUPS[-1],
            held if group is GROUPS[0] else [],
        )

    kept, away = made
    chip = (kept + send(away, flip_pairs(dcore=1)).astype(jnp.float32)).astype(jnp.bfloat16)
    other = send(chip, flip_pairs(dzh=1))

    activation, own_term, back_own, grads, sums = dense_call(
        rep[None], chip, other, features, cotangent, mask, inv_col, inv_row, w_self, w_neigh, bias
    )
    back_got = send(back_own, flip_pairs(dcore=1))

    arrived, extra, products = {}, {}, {}
    for k, after in BACK:
        products[k] = backward_call(
            core[None],
            adjacency[k],
            back_own,
            back_got,
            extra.get(k, []),
            [arrived[a] for a in after],
        )
        moved = send(products[k], [(b, a) for a, b in column_pairs(k)])
        if PLAN[k] is None:
            arrived[k] = moved
        else:
            extra.setdefault(k ^ PLAN[k], []).append(moved)
    waited = [products[k] for k in MADE] + [arrived[k] for k in EARLY]
    grad_self, grad_neigh, grad_bias = weight_grads(
        grads, sums, zh, core, rows * lax.axis_size("blk")
    )

    kept, away = split_call(core[None], list(arrived.values()))
    chip = kept + send(away, flip_pairs(dcore=1)).astype(jnp.float32)
    got = send(pick(chip, 1 - zh).astype(jnp.bfloat16), flip_pairs(dzh=1))
    grad_features = final_call(pick(chip, zh), got, own_term)
    return (activation, grad_features, grad_self, grad_neigh, grad_bias)


def solution(mesh):
    return jax.shard_map(
        shards,
        mesh=mesh,
        in_specs=(
            P("blk", None),
            P("blk", "rep", None, None, None),
            P("blk", "rep", None),
            P("blk", "rep"),
            P("blk"),
            P("blk"),
            P("blk", None),
            P(),
            P(),
            P(),
        ),
        out_specs=(P(("blk", "rep"), None), P(("blk", "rep"), None), P(), P(), P()),
        check_vma=False,
    )
```

```python
import functools

import jax
import jax.numpy as jnp
from jax import lax
from jax.experimental import pallas as pl
from jax.experimental.pallas import tpu as pltpu
from jax.sharding import PartitionSpec as P

AXES = ("blk", "rep")
NB = 8
ND = 8
NS = 6
BS = 128
F = 256
VMEM = 50 * 1024 * 1024
SMALL = 16 * 1024 * 1024
PLAN = {6: None, 3: None, 1: None, 2: None, 0: None, 7: 1, 4: 2, 5: 6}
CROSS = {1: 0x7666, 3: 0x5FDB}
BACK_PLAN = {6: None, 2: None, 1: None, 0: None, 3: 1, 7: 1, 4: 2, 5: 2}
BACK_CROSS = {1: 0xAAAA}
GROUPS = ((6, 3, 1, 2, 0), (7, 4, 5))
HELD = ((6, (1,)), (3, (2, 0)))
BACK = ((5, 3, 4), (1, 0), (7,), (2,), (6,))
LATER = (7, 1)


def index_of(y, x, zl, zh, core):
    return (((y % 4 * 4 + x % 4) * 2 + zl) * 2 + zh) * 2 + core


def places():
    for t in range(128):
        yield t, t >> 5, t >> 3 & 3, t >> 2 & 1, t >> 1 & 1, t & 1


def column_pairs(k, plan, cross):
    via = plan[k]
    out = []
    for t, y, x, zl, zh, core in places():
        j, r = x * 2 + zl, 2 * zh + core
        jj = j ^ k
        if via is None:
            flip = cross[k] >> (jj * 2 + core) & 1 if k & 1 else 0
            out.append((index_of(y - r - (jj > j), jj >> 1, jj & 1, zh ^ flip, core), t))
        else:
            jn = j ^ via
            out.append((index_of(y - (jj > j) + (jj > jn), jn >> 1, jn & 1, zh, core), t))
    return out


def flip_pairs(dy=0, dx=0, dzl=0, dzh=0, dcore=0):
    return [
        (t, index_of(y ^ dy, x ^ dx, zl ^ dzl, zh ^ dzh, core ^ dcore))
        for t, y, x, zl, zh, core in places()
    ]


def send(value, pairs):
    return lax.ppermute(value, AXES, pairs)


def params(limit=VMEM):
    return pltpu.CompilerParams(vmem_limit_bytes=limit)


SMEM = pl.BlockSpec(memory_space=pltpu.SMEM)
HBM = pl.BlockSpec(memory_space=pltpu.HBM)
UNREAD = pl.BlockSpec(memory_space=pl.ANY)
WHOLE = pl.BlockSpec(memory_space=pltpu.VMEM)


def matmul_cost(n):
    return pl.CostEstimate(
        flops=2 * NB * NB * BS * BS * F * n, bytes_accessed=(3 << 20) * n, transcendentals=0
    )


def assemble_body(n, sel_ref, cols_ref, counts_ref, tiles_ref, out_ref, held_ref, made_ref, sems):
    def fetch(k):
        dist, slot = sel_ref[k], k % 2
        return pltpu.make_async_copy(tiles_ref.at[:, dist], held_ref.at[slot], sems.at[0, slot])

    def store(k):
        return pltpu.make_async_copy(made_ref.at[k % 2], out_ref.at[k], sems.at[1, k % 2])

    fetch(0).start()
    for k in range(n):
        fetch(k).wait()
        if k + 1 < n:
            fetch(k + 1).start()
        if k > 1:
            store(k - 2).wait()
        dist, slot = sel_ref[k], k % 2

        def block_row(b, carry):
            count = counts_ref[b * ND + dist]
            rows = pl.ds(pl.multiple_of(b * BS, BS), BS)
            cols = [cols_ref[(b * ND + dist) * NS + s] for s in range(NS)]
            cols = [jnp.where(s < count, cols[s], NB) for s in range(NS)]
            tiles = [held_ref[slot, b, s] for s in range(NS)]
            zero = jnp.zeros((BS, BS), jnp.bfloat16)
            for c in range(NB):
                parts = [jnp.where(cols[s] == c, tiles[s], zero) for s in range(NS)]
                pairs = [parts[s] + parts[s + 1] for s in range(0, NS, 2)]
                made_ref[slot, c, rows, :] = pairs[0] + pairs[1] + pairs[2]
            return carry

        lax.fori_loop(0, NB, block_row, 0)
        store(k).start()
    store(n - 2).wait()
    store(n - 1).wait()


def assemble_call(sel, cols, counts, tiles):
    n = sel.shape[0]
    return pl.pallas_call(
        functools.partial(assemble_body, n),
        out_shape=jax.ShapeDtypeStruct((n, NB, NB * BS, BS), jnp.bfloat16),
        in_specs=[SMEM] * 3 + [HBM],
        out_specs=HBM,
        scratch_shapes=[
            pltpu.VMEM((2, NB, NS, BS, BS), jnp.bfloat16),
            pltpu.VMEM((2, NB, NB * BS, BS), jnp.bfloat16),
            pltpu.SemaphoreType.DMA((2, 2)),
        ],
        compiler_params=params(),
        cost_estimate=matmul_cost(n),
        name="assemble_adjacency",
    )(sel, cols, counts, tiles)


def copies_of(adj_ref, places, held_ref, sems):
    copies = [
        pltpu.make_async_copy(adj_ref.at[place], held_ref.at[k], sems.at[k])
        for k, place in enumerate(places)
    ]
    for copy in copies:
        copy.start()
    return copies


def copy_scratch(n):
    return [
        pltpu.VMEM((n, NB, NB * BS, BS), jnp.bfloat16),
        pltpu.SemaphoreType.DMA((n,)),
    ]


def wide(ref, k):
    return jnp.concatenate([ref[k, c] for c in range(NB)], 1)


def forward_body(n, start, first, last, core_ref, adj_ref, *refs):
    shards, rest = refs[:n], refs[n:]
    total_ref, held_ref, sems = rest[-3:]
    outs = rest[-5:-3] if last else rest[-4:-3]
    copies = copies_of(adj_ref, range(start, start + n), held_ref, sems)
    for k in range(n):
        copies[k].wait()
        product = jnp.dot(wide(held_ref, k), shards[k][...], preferred_element_type=jnp.float32)
        if k > 0:
            total_ref[...] += product
        else:
            total_ref[...] = product if first else rest[0][...] + product
    if last:
        core = core_ref[0]
        for part in range(2):
            keep = pl.multiple_of((part * 2 + core) * 256, 256)
            away = pl.multiple_of((part * 2 + 1 - core) * 256, 256)
            outs[0][part] = total_ref[pl.ds(keep, 256), :]
            outs[1][part] = total_ref[pl.ds(away, 256), :].astype(jnp.bfloat16)
    else:
        outs[0][...] = total_ref[...]


def forward_call(core, adjacency, start, shards, before, last, after):
    n, first = len(shards), before is None
    if last:
        out_shape = (
            jax.ShapeDtypeStruct((2, 256, F), jnp.float32),
            jax.ShapeDtypeStruct((2, 256, F), jnp.bfloat16),
        )
    else:
        out_shape = (jax.ShapeDtypeStruct((NB * BS, F), jnp.float32),)
    return pl.pallas_call(
        functools.partial(forward_body, n, start, first, last),
        out_shape=out_shape,
        in_specs=[SMEM, HBM] + [WHOLE] * (n + (not first)) + [UNREAD] * len(after),
        out_specs=(WHOLE,) * len(out_shape),
        scratch_shapes=[pltpu.VMEM((NB * BS, F), jnp.float32)] + copy_scratch(n),
        compiler_params=params(),
        cost_estimate=matmul_cost(n),
        name="forward_product",
    )(core, adjacency, *shards, *([] if first else [before]), *after)


def dense_body(
    rep_ref, own_ref, got_ref, feat_ref, cot_ref, inv_ref, ws_ref, wn_ref, bias_ref,
    act_ref, term_ref, back_ref, grad_ref,
):
    zh = rep_ref[0] // 2
    nt = (((1,), (1,)), ((), ()))
    tn = (((0,), (0,)), ((), ()))
    grads = jnp.zeros((F, F), jnp.float32)
    sums = jnp.zeros((1, F), jnp.float32)
    for part in range(2):
        feat = feat_ref[part]
        inv = inv_ref[part]
        summed = own_ref[part].astype(jnp.float32) + got_ref[part].astype(jnp.float32)
        agg = (summed * jnp.broadcast_to(inv, (256, 256)).T).astype(jnp.bfloat16)
        pre = (
            jnp.dot(feat, ws_ref[...], preferred_element_type=jnp.float32)
            + jnp.dot(agg, wn_ref[...], preferred_element_type=jnp.float32)
            + bias_ref[...]
        )
        sigm = jax.nn.sigmoid(pre)
        act = (pre * sigm).astype(jnp.bfloat16)
        slope = sigm * (1.0 + pre * (1.0 - sigm))
        grad_pre = (cot_ref[part].astype(jnp.float32) * slope).astype(jnp.bfloat16)

        @pl.when(zh == part)
        def _():
            act_ref[...] = act
            term_ref[...] = lax.dot_general(
                grad_pre, ws_ref[...], nt, preferred_element_type=jnp.float32
            )

        back_t = lax.dot_general(wn_ref[...], grad_pre, nt, preferred_element_type=jnp.float32)
        back_ref[part] = (back_t * inv).astype(jnp.bfloat16)
        left = jnp.where(zh == 0, feat, agg)
        grads += lax.dot_general(left, grad_pre, tn, preferred_element_type=jnp.float32)
        sums += jnp.sum(grad_pre.astype(jnp.float32), axis=0, keepdims=True)
    grad_ref[:F, :] = grads
    grad_ref[F:, :] = jnp.broadcast_to(sums, (8, F))


def dense_call(rep, own, got, feat, cot, inv, w_self, w_neigh, bias):
    return pl.pallas_call(
        dense_body,
        out_shape=(
            jax.ShapeDtypeStruct((256, F), jnp.bfloat16),
            jax.ShapeDtypeStruct((256, F), jnp.float32),
            jax.ShapeDtypeStruct((2, F, 256), jnp.bfloat16),
            jax.ShapeDtypeStruct((F + 8, F), jnp.float32),
        ),
        in_specs=[SMEM] + [WHOLE] * 8,
        out_specs=(WHOLE,) * 4,
        compiler_params=params(SMALL),
        name="dense_rows",
    )(rep, own, got, feat, cot, inv, w_self, w_neigh, bias)


def backward_body(places, added, core_ref, adj_ref, own_ref, got_ref, *rest):
    n = len(places)
    held_ref, sems = rest[-2:]
    outs = rest[-2 - n : -2]
    copies = copies_of(adj_ref, places, held_ref, sems)
    core = core_ref[0]
    message = []
    for quarter in range(4):
        mine = core == quarter % 2
        message.append(jnp.where(mine, own_ref[quarter // 2], got_ref[quarter // 2]))
    message = jnp.concatenate(message, 1)
    for k in range(n):
        copies[k].wait()
        product = jnp.dot(message, wide(held_ref, k), preferred_element_type=jnp.float32)
        for c in range(NB):
            part = product[:, c * BS : (c + 1) * BS]
            for ref in rest[:added]:
                part += ref[c].astype(jnp.float32)
            outs[k][c] = part.astype(jnp.bfloat16)


def backward_call(core, adjacency, places, own, got, extra, after):
    n, added = len(places), len(extra)
    return pl.pallas_call(
        functools.partial(backward_body, tuple(places), added),
        out_shape=(jax.ShapeDtypeStruct((NB, F, BS), jnp.bfloat16),) * n,
        in_specs=[SMEM, HBM] + [WHOLE] * (2 + added) + [UNREAD] * len(after),
        out_specs=(WHOLE,) * n,
        scratch_shapes=copy_scratch(n),
        compiler_params=params(),
        cost_estimate=matmul_cost(n),
        name="backward_product",
    )(core, adjacency, own, got, *extra, *after)


def split_body(core_ref, *rest):
    arrived, (keep_ref, away_ref) = rest[:-2], rest[-2:]
    core = core_ref[0]
    for part in range(2):
        for c in range(2):
            keep = (part * 2 + core) * 2 + c
            away = (part * 2 + 1 - core) * 2 + c
            kept = arrived[0][keep].astype(jnp.float32)
            sent = arrived[0][away].astype(jnp.float32)
            for ref in arrived[1:]:
                kept += ref[keep].astype(jnp.float32)
                sent += ref[away].astype(jnp.float32)
            keep_ref[part, c] = kept
            away_ref[part, c] = sent.astype(jnp.bfloat16)


def split_call(core, arrived):
    return pl.pallas_call(
        split_body,
        out_shape=(
            jax.ShapeDtypeStruct((2, 2, F, BS), jnp.float32),
            jax.ShapeDtypeStruct((2, 2, F, BS), jnp.bfloat16),
        ),
        in_specs=[SMEM] + [WHOLE] * len(arrived),
        out_specs=(WHOLE, WHOLE),
        compiler_params=params(SMALL),
        name="split_products",
    )(core, *arrived)


def hold_body(*refs):
    pass


def hold_call(along, after):
    return pl.pallas_call(
        hold_body,
        out_shape=jax.ShapeDtypeStruct(along.shape, along.dtype),
        in_specs=[UNREAD] * (1 + len(after)),
        out_specs=UNREAD,
        input_output_aliases={0: 0},
        name="hold",
    )(along, *after)


def final_body(kept_ref, got_ref, term_ref, out_ref):
    for c in range(2):
        spread = kept_ref[c] + got_ref[c].astype(jnp.float32)
        rows = slice(c * BS, (c + 1) * BS)
        out_ref[rows, :] = (term_ref[rows, :] + spread.T).astype(jnp.bfloat16)


def final_call(kept, got, term):
    return pl.pallas_call(
        final_body,
        out_shape=jax.ShapeDtypeStruct((256, F), jnp.bfloat16),
        compiler_params=params(SMALL),
        name="final_rows",
    )(kept, got, term)


def pick(pair, index):
    return lax.dynamic_index_in_dim(pair, index, 0, keepdims=False)


def weight_shares(grads, core):
    halves, sums = grads[:F].reshape(2, F // 2, F), grads[F:]
    away = jnp.concatenate([pick(halves, 1 - core), sums], 0)
    mine = jnp.concatenate([pick(halves, core), sums], 0) + send(away, flip_pairs(dcore=1))
    count = lax.axis_size("blk")
    bias = mine[F // 2 : F // 2 + 1]
    high = bias.astype(jnp.bfloat16)
    low = (bias - high.astype(jnp.float32)).astype(jnp.bfloat16)
    bias_rows = jnp.broadcast_to(jnp.concatenate([high, low], 0)[None], (count, 2, F))
    rows = mine[: F // 2].astype(jnp.bfloat16).reshape(count, F // 2 // count, F)
    return lax.all_to_all(jnp.concatenate([rows, bias_rows], 1), "blk", 0, 0)


def weight_grads(parts, zh, core, nodes):
    count, share = parts.shape[0], parts.shape[1] - 2
    total = jnp.sum(parts.astype(jnp.float32), axis=0)
    bias = total[share] + total[share + 1]
    spread = jnp.broadcast_to(total[None, :share], (count, share, F))
    half = lax.all_to_all(spread, "blk", 0, 0).reshape(F // 2, F)
    other = send(half, flip_pairs(dzh=1))
    both = jnp.where(zh == 0, jnp.stack([half, other]), jnp.stack([other, half]))
    across = send(both, flip_pairs(dcore=1))
    low, top = jnp.where(core == 0, both, across), jnp.where(core == 0, across, both)
    norm = 1.0 / jnp.sqrt(jnp.float32(nodes))
    whole = jnp.concatenate([low, top], 1) * norm
    return whole[0], whole[1], bias * norm


def shards(
    features, tiles, tile_cols, counts, degree, train_mask, cotangent, w_self, w_neigh, bias_term
):
    rows = features.shape[0]
    rep = lax.axis_index("rep").astype(jnp.int32)
    zh, core = rep // 2, rep % 2
    place = (lax.axis_index("blk") % 8).astype(jnp.int32)
    cols = tile_cols.reshape(-1)
    live = counts.reshape(-1)

    def distance_of(k):
        return (place - (place ^ k)) % 8

    def own_rows(value):
        value = value.reshape((2, 2, rows // 4) + value.shape[1:])
        return lax.dynamic_index_in_dim(value, core, 1, keepdims=False)

    inv = own_rows(1.0 / degree.astype(jnp.float32))[:, None, :]
    feat = own_rows(features)
    cot = own_rows(cotangent) * own_rows(train_mask).astype(jnp.bfloat16)[:, :, None]
    bias = bias_term.reshape(1, F)

    order = list(PLAN)
    sel = jnp.stack([distance_of(k) for k in order])
    adjacency = assemble_call(sel, cols, live, tiles)
    blocks, held = {}, []
    for k, via in PLAN.items():
        if via is None:
            blocks[k] = send(features, column_pairs(k, PLAN, CROSS))
    for k, after in HELD:
        blocks[k] = hold_call(blocks[k], [adjacency] + [blocks[a] for a in after])
        held.append(blocks[k])
    for k, via in PLAN.items():
        if via is not None:
            blocks[k] = send(blocks[k ^ via], column_pairs(k, PLAN, CROSS))
    made = (None,)
    for group in GROUPS:
        made = forward_call(
            core[None],
            adjacency,
            order.index(group[0]),
            [blocks[k] for k in group],
            made[0],
            group is GROUPS[-1],
            held if group is GROUPS[0] else [],
        )

    kept, away = made
    chip = (kept + send(away, flip_pairs(dcore=1)).astype(jnp.float32)).astype(jnp.bfloat16)
    other = send(chip, flip_pairs(dzh=1))

    activation, own_term, back_own, grads = dense_call(
        rep[None], chip, other, feat, cot, inv, w_self, w_neigh, bias
    )
    back_got = send(back_own, flip_pairs(dcore=1))

    parts = weight_shares(grads, core)
    arrived, extra = {}, {}
    for group in BACK:
        made = backward_call(
            core[None],
            adjacency,
            [order.index(k) for k in group],
            back_own,
            back_got,
            extra.get(group[0], []),
            [parts] if group[0] in LATER else [],
        )
        for k, product in zip(group, made):
            pairs = column_pairs(k, BACK_PLAN, BACK_CROSS)
            moved = send(product, [(b, a) for a, b in pairs])
            if BACK_PLAN[k] is None:
                arrived[k] = moved
            else:
                extra.setdefault(k ^ BACK_PLAN[k], []).append(moved)
    kept, away = split_call(core[None], list(arrived.values()))
    chip = kept + send(away, flip_pairs(dcore=1)).astype(jnp.float32)
    got = send(pick(chip, 1 - zh).astype(jnp.bfloat16), flip_pairs(dzh=1))
    grad_features = final_call(pick(chip, zh), got, own_term)
    grad_self, grad_neigh, grad_bias = weight_grads(
        parts, zh, core, rows * lax.axis_size("blk")
    )
    return (activation, grad_features, grad_self, grad_neigh, grad_bias)


def solution(mesh):
    return jax.shard_map(
        shards,
        mesh=mesh,
        in_specs=(
            P("blk", None),
            P("blk", "rep", None, None, None),
            P("blk", "rep", None),
            P("blk", "rep"),
            P("blk"),
            P("blk"),
            P("blk", None),
            P(),
            P(),
            P(),
        ),
        out_specs=(P(("blk", "rep"), None), P(("blk", "rep"), None), P(), P(), P()),
        check_vma=False,
    )
```

```python
import functools

import jax
import jax.numpy as jnp
from jax import lax
from jax.experimental import pallas as pl
from jax.experimental.pallas import tpu as pltpu
from jax.sharding import PartitionSpec as P

AXES = ("blk", "rep")
NB = 8
ND = 8
NS = 6
BS = 128
F = 256
VMEM = 50 * 1024 * 1024
SMALL = 16 * 1024 * 1024
PLAN = {6: None, 3: None, 1: None, 2: None, 0: None, 7: 1, 4: 2, 5: 6}
CROSS = {1: 0x7666, 3: 0x5FDB}
BACK_PLAN = {6: None, 1: None, 0: None, 2: 2, 3: 1, 7: 1, 4: 2, 5: 2}
BACK_CROSS = {1: 0xAAAA}
GROUPS = ((6, 3, 1, 2, 0), (7, 4, 5))
HELD = ((6, (1,)), (3, (2, 0)))
BACK = ((5, 3, 4, 1), (7,), (2,), (6,), (0,))
LATER = (7,)


def index_of(y, x, zl, zh, core):
    return (((y % 4 * 4 + x % 4) * 2 + zl) * 2 + zh) * 2 + core


def places():
    for t in range(128):
        yield t, t >> 5, t >> 3 & 3, t >> 2 & 1, t >> 1 & 1, t & 1


def column_pairs(k, plan, cross):
    via = plan[k]
    out = []
    for t, y, x, zl, zh, core in places():
        j, r = x * 2 + zl, 2 * zh + core
        jj = j ^ k
        if via is None:
            flip = cross[k] >> (jj * 2 + core) & 1 if k & 1 else 0
            out.append((index_of(y - r - (jj > j), jj >> 1, jj & 1, zh ^ flip, core), t))
        else:
            jn = j ^ via
            out.append((index_of(y - (jj > j) + (jj > jn), jn >> 1, jn & 1, zh, core), t))
    return out


def flip_pairs(dy=0, dx=0, dzl=0, dzh=0, dcore=0):
    return [
        (t, index_of(y ^ dy, x ^ dx, zl ^ dzl, zh ^ dzh, core ^ dcore))
        for t, y, x, zl, zh, core in places()
    ]


def send(value, pairs):
    return lax.ppermute(value, AXES, pairs)


def params(limit=VMEM):
    return pltpu.CompilerParams(vmem_limit_bytes=limit)


SMEM = pl.BlockSpec(memory_space=pltpu.SMEM)
HBM = pl.BlockSpec(memory_space=pltpu.HBM)
UNREAD = pl.BlockSpec(memory_space=pl.ANY)
WHOLE = pl.BlockSpec(memory_space=pltpu.VMEM)


def matmul_cost(n):
    return pl.CostEstimate(
        flops=2 * NB * NB * BS * BS * F * n, bytes_accessed=(3 << 20) * n, transcendentals=0
    )


def assemble_body(n, sel_ref, cols_ref, counts_ref, tiles_ref, out_ref, held_ref, made_ref, sems):
    def fetch(k):
        dist, slot = sel_ref[k], k % 2
        return pltpu.make_async_copy(tiles_ref.at[:, dist], held_ref.at[slot], sems.at[0, slot])

    def store(k):
        return pltpu.make_async_copy(made_ref.at[k % 2], out_ref.at[k], sems.at[1, k % 2])

    fetch(0).start()
    for k in range(n):
        fetch(k).wait()
        if k + 1 < n:
            fetch(k + 1).start()
        if k > 1:
            store(k - 2).wait()
        dist, slot = sel_ref[k], k % 2

        def block_row(b, carry):
            count = counts_ref[b * ND + dist]
            rows = pl.ds(pl.multiple_of(b * BS, BS), BS)
            cols = [cols_ref[(b * ND + dist) * NS + s] for s in range(NS)]
            cols = [jnp.where(s < count, cols[s], NB) for s in range(NS)]
            tiles = [held_ref[slot, b, s] for s in range(NS)]
            zero = jnp.zeros((BS, BS), jnp.bfloat16)
            for c in range(NB):
                parts = [jnp.where(cols[s] == c, tiles[s], zero) for s in range(NS)]
                pairs = [parts[s] + parts[s + 1] for s in range(0, NS, 2)]
                made_ref[slot, c, rows, :] = pairs[0] + pairs[1] + pairs[2]
            return carry

        lax.fori_loop(0, NB, block_row, 0)
        store(k).start()
    store(n - 2).wait()
    store(n - 1).wait()


def assemble_call(sel, cols, counts, tiles):
    n = sel.shape[0]
    return pl.pallas_call(
        functools.partial(assemble_body, n),
        out_shape=jax.ShapeDtypeStruct((n, NB, NB * BS, BS), jnp.bfloat16),
        in_specs=[SMEM] * 3 + [HBM],
        out_specs=HBM,
        scratch_shapes=[
            pltpu.VMEM((2, NB, NS, BS, BS), jnp.bfloat16),
            pltpu.VMEM((2, NB, NB * BS, BS), jnp.bfloat16),
            pltpu.SemaphoreType.DMA((2, 2)),
        ],
        compiler_params=params(),
        cost_estimate=matmul_cost(n),
        name="assemble_adjacency",
    )(sel, cols, counts, tiles)


def copies_of(adj_ref, places, held_ref, sems):
    copies = [
        pltpu.make_async_copy(adj_ref.at[place], held_ref.at[k], sems.at[k])
        for k, place in enumerate(places)
    ]
    for copy in copies:
        copy.start()
    return copies


def copy_scratch(n):
    return [
        pltpu.VMEM((n, NB, NB * BS, BS), jnp.bfloat16),
        pltpu.SemaphoreType.DMA((n,)),
    ]


def wide(ref, k):
    return jnp.concatenate([ref[k, c] for c in range(NB)], 1)


def forward_body(n, start, first, last, core_ref, adj_ref, *refs):
    shards, rest = refs[:n], refs[n:]
    total_ref, held_ref, sems = rest[-3:]
    outs = rest[-5:-3] if last else rest[-4:-3]
    copies = copies_of(adj_ref, range(start, start + n), held_ref, sems)
    for k in range(n):
        copies[k].wait()
        product = jnp.dot(wide(held_ref, k), shards[k][...], preferred_element_type=jnp.float32)
        if k > 0:
            total_ref[...] += product
        else:
            total_ref[...] = product if first else rest[0][...] + product
    if last:
        core = core_ref[0]
        for part in range(2):
            keep = pl.multiple_of((part * 2 + core) * 256, 256)
            away = pl.multiple_of((part * 2 + 1 - core) * 256, 256)
            outs[0][part] = total_ref[pl.ds(keep, 256), :]
            outs[1][part] = total_ref[pl.ds(away, 256), :].astype(jnp.bfloat16)
    else:
        outs[0][...] = total_ref[...]


def forward_call(core, adjacency, start, shards, before, last, after):
    n, first = len(shards), before is None
    if last:
        out_shape = (
            jax.ShapeDtypeStruct((2, 256, F), jnp.float32),
            jax.ShapeDtypeStruct((2, 256, F), jnp.bfloat16),
        )
    else:
        out_shape = (jax.ShapeDtypeStruct((NB * BS, F), jnp.float32),)
    return pl.pallas_call(
        functools.partial(forward_body, n, start, first, last),
        out_shape=out_shape,
        in_specs=[SMEM, HBM] + [WHOLE] * (n + (not first)) + [UNREAD] * len(after),
        out_specs=(WHOLE,) * len(out_shape),
        scratch_shapes=[pltpu.VMEM((NB * BS, F), jnp.float32)] + copy_scratch(n),
        compiler_params=params(),
        cost_estimate=matmul_cost(n),
        name="forward_product",
    )(core, adjacency, *shards, *([] if first else [before]), *after)


def dense_body(
    rep_ref, own_ref, got_ref, feat_ref, cot_ref, inv_ref, ws_ref, wn_ref, bias_ref,
    act_ref, term_ref, back_ref, grad_ref,
):
    zh = rep_ref[0] // 2
    nt = (((1,), (1,)), ((), ()))
    tn = (((0,), (0,)), ((), ()))
    grads = jnp.zeros((F, F), jnp.float32)
    sums = jnp.zeros((1, F), jnp.float32)
    for part in range(2):
        feat = feat_ref[part]
        inv = inv_ref[part]
        summed = own_ref[part].astype(jnp.float32) + got_ref[part].astype(jnp.float32)
        agg = (summed * jnp.broadcast_to(inv, (256, 256)).T).astype(jnp.bfloat16)
        pre = (
            jnp.dot(feat, ws_ref[...], preferred_element_type=jnp.float32)
            + jnp.dot(agg, wn_ref[...], preferred_element_type=jnp.float32)
            + bias_ref[...]
        )
        sigm = jax.nn.sigmoid(pre)
        act = (pre * sigm).astype(jnp.bfloat16)
        slope = sigm * (1.0 + pre * (1.0 - sigm))
        grad_pre = (cot_ref[part].astype(jnp.float32) * slope).astype(jnp.bfloat16)

        @pl.when(zh == part)
        def _():
            act_ref[...] = act
            term_ref[...] = lax.dot_general(
                grad_pre, ws_ref[...], nt, preferred_element_type=jnp.float32
            )

        back_t = lax.dot_general(wn_ref[...], grad_pre, nt, preferred_element_type=jnp.float32)
        back_ref[part] = (back_t * inv).astype(jnp.bfloat16)
        left = jnp.where(zh == 0, feat, agg)
        grads += lax.dot_general(left, grad_pre, tn, preferred_element_type=jnp.float32)
        sums += jnp.sum(grad_pre.astype(jnp.float32), axis=0, keepdims=True)
    grad_ref[:F, :] = grads
    grad_ref[F:, :] = jnp.broadcast_to(sums, (8, F))


def dense_call(rep, own, got, feat, cot, inv, w_self, w_neigh, bias):
    return pl.pallas_call(
        dense_body,
        out_shape=(
            jax.ShapeDtypeStruct((256, F), jnp.bfloat16),
            jax.ShapeDtypeStruct((256, F), jnp.float32),
            jax.ShapeDtypeStruct((2, F, 256), jnp.bfloat16),
            jax.ShapeDtypeStruct((F + 8, F), jnp.float32),
        ),
        in_specs=[SMEM] + [WHOLE] * 8,
        out_specs=(WHOLE,) * 4,
        compiler_params=params(SMALL),
        name="dense_rows",
    )(rep, own, got, feat, cot, inv, w_self, w_neigh, bias)


def backward_body(places, added, core_ref, adj_ref, own_ref, got_ref, *rest):
    n = len(places)
    held_ref, sems = rest[-2:]
    outs = rest[-2 - n : -2]
    copies = copies_of(adj_ref, places, held_ref, sems)
    core = core_ref[0]
    message = []
    for quarter in range(4):
        mine = core == quarter % 2
        message.append(jnp.where(mine, own_ref[quarter // 2], got_ref[quarter // 2]))
    message = jnp.concatenate(message, 1)
    for k in range(n):
        copies[k].wait()
        product = jnp.dot(message, wide(held_ref, k), preferred_element_type=jnp.float32)
        for c in range(NB):
            part = product[:, c * BS : (c + 1) * BS]
            for ref in rest[:added]:
                part += ref[c].astype(jnp.float32)
            outs[k][c] = part.astype(jnp.bfloat16)


def backward_call(core, adjacency, places, own, got, extra, after):
    n, added = len(places), len(extra)
    return pl.pallas_call(
        functools.partial(backward_body, tuple(places), added),
        out_shape=(jax.ShapeDtypeStruct((NB, F, BS), jnp.bfloat16),) * n,
        in_specs=[SMEM, HBM] + [WHOLE] * (2 + added) + [UNREAD] * len(after),
        out_specs=(WHOLE,) * n,
        scratch_shapes=copy_scratch(n),
        compiler_params=params(),
        cost_estimate=matmul_cost(n),
        name="backward_product",
    )(core, adjacency, own, got, *extra, *after)


def split_body(core_ref, *rest):
    arrived, (keep_ref, away_ref) = rest[:-2], rest[-2:]
    core = core_ref[0]
    for part in range(2):
        for c in range(2):
            keep = (part * 2 + core) * 2 + c
            away = (part * 2 + 1 - core) * 2 + c
            kept = arrived[0][keep].astype(jnp.float32)
            sent = arrived[0][away].astype(jnp.float32)
            for ref in arrived[1:]:
                kept += ref[keep].astype(jnp.float32)
                sent += ref[away].astype(jnp.float32)
            keep_ref[part, c] = kept
            away_ref[part, c] = sent.astype(jnp.bfloat16)


def split_call(core, arrived):
    return pl.pallas_call(
        split_body,
        out_shape=(
            jax.ShapeDtypeStruct((2, 2, F, BS), jnp.float32),
            jax.ShapeDtypeStruct((2, 2, F, BS), jnp.bfloat16),
        ),
        in_specs=[SMEM] + [WHOLE] * len(arrived),
        out_specs=(WHOLE, WHOLE),
        compiler_params=params(SMALL),
        name="split_products",
    )(core, *arrived)


def hold_body(*refs):
    pass


def hold_call(along, after):
    return pl.pallas_call(
        hold_body,
        out_shape=jax.ShapeDtypeStruct(along.shape, along.dtype),
        in_specs=[UNREAD] * (1 + len(after)),
        out_specs=UNREAD,
        input_output_aliases={0: 0},
        name="hold",
    )(along, *after)


def final_body(kept_ref, got_ref, term_ref, out_ref):
    for c in range(2):
        spread = kept_ref[c] + got_ref[c].astype(jnp.float32)
        rows = slice(c * BS, (c + 1) * BS)
        out_ref[rows, :] = (term_ref[rows, :] + spread.T).astype(jnp.bfloat16)


def final_call(kept, got, term):
    return pl.pallas_call(
        final_body,
        out_shape=jax.ShapeDtypeStruct((256, F), jnp.bfloat16),
        compiler_params=params(SMALL),
        name="final_rows",
    )(kept, got, term)


def pick(pair, index):
    return lax.dynamic_index_in_dim(pair, index, 0, keepdims=False)


def weight_shares(grads, core):
    halves, sums = grads[:F].reshape(2, F // 2, F), grads[F:]
    away = jnp.concatenate([pick(halves, 1 - core), sums], 0)
    mine = jnp.concatenate([pick(halves, core), sums], 0) + send(away, flip_pairs(dcore=1))
    count = lax.axis_size("blk")
    bias = mine[F // 2 : F // 2 + 1]
    high = bias.astype(jnp.bfloat16)
    low = (bias - high.astype(jnp.float32)).astype(jnp.bfloat16)
    bias_rows = jnp.broadcast_to(jnp.concatenate([high, low], 0)[None], (count, 2, F))
    rows = mine[: F // 2].astype(jnp.bfloat16).reshape(count, F // 2 // count, F)
    return lax.all_to_all(jnp.concatenate([rows, bias_rows], 1), "blk", 0, 0)


def weight_grads(parts, zh, core, nodes):
    count, share = parts.shape[0], parts.shape[1] - 2
    total = jnp.sum(parts.astype(jnp.float32), axis=0)
    bias = total[share] + total[share + 1]
    spread = jnp.broadcast_to(total[None, :share], (count, share, F))
    half = lax.all_to_all(spread, "blk", 0, 0).reshape(F // 2, F)
    other = send(half, flip_pairs(dzh=1))
    both = jnp.where(zh == 0, jnp.stack([half, other]), jnp.stack([other, half]))
    across = send(both, flip_pairs(dcore=1))
    low, top = jnp.where(core == 0, both, across), jnp.where(core == 0, across, both)
    norm = 1.0 / jnp.sqrt(jnp.float32(nodes))
    whole = jnp.concatenate([low, top], 1) * norm
    return whole[0], whole[1], bias * norm


def shards(
    features, tiles, tile_cols, counts, degree, train_mask, cotangent, w_self, w_neigh, bias_term
):
    rows = features.shape[0]
    rep = lax.axis_index("rep").astype(jnp.int32)
    zh, core = rep // 2, rep % 2
    place = (lax.axis_index("blk") % 8).astype(jnp.int32)
    cols = tile_cols.reshape(-1)
    live = counts.reshape(-1)

    def distance_of(k):
        return (place - (place ^ k)) % 8

    def own_rows(value):
        value = value.reshape((2, 2, rows // 4) + value.shape[1:])
        return lax.dynamic_index_in_dim(value, core, 1, keepdims=False)

    inv = own_rows(1.0 / degree.astype(jnp.float32))[:, None, :]
    feat = own_rows(features)
    cot = own_rows(cotangent) * own_rows(train_mask).astype(jnp.bfloat16)[:, :, None]
    bias = bias_term.reshape(1, F)

    order = list(PLAN)
    sel = jnp.stack([distance_of(k) for k in order])
    adjacency = assemble_call(sel, cols, live, tiles)
    blocks, held = {}, []
    for k, via in PLAN.items():
        if via is None:
            blocks[k] = send(features, column_pairs(k, PLAN, CROSS))
    for k, after in HELD:
        blocks[k] = hold_call(blocks[k], [adjacency] + [blocks[a] for a in after])
        held.append(blocks[k])
    for k, via in PLAN.items():
        if via is not None:
            blocks[k] = send(blocks[k ^ via], column_pairs(k, PLAN, CROSS))
    made = (None,)
    for group in GROUPS:
        made = forward_call(
            core[None],
            adjacency,
            order.index(group[0]),
            [blocks[k] for k in group],
            made[0],
            group is GROUPS[-1],
            held if group is GROUPS[0] else [],
        )

    kept, away = made
    chip = (kept + send(away, flip_pairs(dcore=1)).astype(jnp.float32)).astype(jnp.bfloat16)
    other = send(chip, flip_pairs(dzh=1))

    activation, own_term, back_own, grads = dense_call(
        rep[None], chip, other, feat, cot, inv, w_self, w_neigh, bias
    )
    back_got = send(back_own, flip_pairs(dcore=1))

    parts = weight_shares(grads, core)
    arrived, extra = {}, {}
    for group in BACK:
        made = backward_call(
            core[None],
            adjacency,
            [order.index(k) for k in group],
            back_own,
            back_got,
            extra.get(group[0], []),
            [parts] if group[0] in LATER else [],
        )
        for k, product in zip(group, made):
            pairs = column_pairs(k, BACK_PLAN, BACK_CROSS)
            moved = send(product, [(b, a) for a, b in pairs])
            if BACK_PLAN[k] is None:
                arrived[k] = moved
            else:
                extra.setdefault(k ^ BACK_PLAN[k], []).append(moved)
    kept, away = split_call(core[None], list(arrived.values()))
    chip = kept + send(away, flip_pairs(dcore=1)).astype(jnp.float32)
    got = send(pick(chip, 1 - zh).astype(jnp.bfloat16), flip_pairs(dzh=1))
    grad_features = final_call(pick(chip, zh), got, own_term)
    grad_self, grad_neigh, grad_bias = weight_grads(
        parts, zh, core, rows * lax.axis_size("blk")
    )
    return (activation, grad_features, grad_self, grad_neigh, grad_bias)


def solution(mesh):
    return jax.shard_map(
        shards,
        mesh=mesh,
        in_specs=(
            P("blk", None),
            P("blk", "rep", None, None, None),
            P("blk", "rep", None),
            P("blk", "rep"),
            P("blk"),
            P("blk"),
            P("blk", None),
            P(),
            P(),
            P(),
        ),
        out_specs=(P(("blk", "rep"), None), P(("blk", "rep"), None), P(), P(), P()),
        check_vma=False,
    )
```

```python
import functools

import jax
import jax.numpy as jnp
from jax import lax
from jax.experimental import pallas as pl
from jax.experimental.pallas import tpu as pltpu
from jax.sharding import PartitionSpec as P

AXES = ("blk", "rep")
NB = 8
ND = 8
NS = 6
BS = 128
F = 256
VMEM = 50 * 1024 * 1024
SMALL = 16 * 1024 * 1024
PLAN = {6: None, 3: None, 1: None, 2: None, 0: None, 7: 1, 4: 2, 5: 6}
CROSS = {1: 0x7666, 3: 0x5FDB}
BACK_PLAN = {6: None, 1: None, 0: None, 2: 2, 3: 1, 7: 1, 4: 2, 5: 2}
BACK_CROSS = {1: 0xAAAA}
GROUPS = ((6, 3, 1, 2, 0), (7, 4, 5))
HELD = ((6, (1,)), (3, (2, 0)))
BACK = ((5, 3, 4, 1), (7,), (2,), (6,), (0,))
LATER = (2,)


def index_of(y, x, zl, zh, core):
    return (((y % 4 * 4 + x % 4) * 2 + zl) * 2 + zh) * 2 + core


def places():
    for t in range(128):
        yield t, t >> 5, t >> 3 & 3, t >> 2 & 1, t >> 1 & 1, t & 1


def column_pairs(k, plan, cross):
    via = plan[k]
    out = []
    for t, y, x, zl, zh, core in places():
        j, r = x * 2 + zl, 2 * zh + core
        jj = j ^ k
        if via is None:
            flip = cross[k] >> (jj * 2 + core) & 1 if k & 1 else 0
            out.append((index_of(y - r - (jj > j), jj >> 1, jj & 1, zh ^ flip, core), t))
        else:
            jn = j ^ via
            out.append((index_of(y - (jj > j) + (jj > jn), jn >> 1, jn & 1, zh, core), t))
    return out


def flip_pairs(dy=0, dx=0, dzl=0, dzh=0, dcore=0):
    return [
        (t, index_of(y ^ dy, x ^ dx, zl ^ dzl, zh ^ dzh, core ^ dcore))
        for t, y, x, zl, zh, core in places()
    ]


def send(value, pairs):
    return lax.ppermute(value, AXES, pairs)


def params(limit=VMEM):
    return pltpu.CompilerParams(vmem_limit_bytes=limit)


SMEM = pl.BlockSpec(memory_space=pltpu.SMEM)
HBM = pl.BlockSpec(memory_space=pltpu.HBM)
UNREAD = pl.BlockSpec(memory_space=pl.ANY)
WHOLE = pl.BlockSpec(memory_space=pltpu.VMEM)


def matmul_cost(n):
    return pl.CostEstimate(
        flops=2 * NB * NB * BS * BS * F * n, bytes_accessed=(3 << 20) * n, transcendentals=0
    )


def assemble_body(n, sel_ref, cols_ref, counts_ref, tiles_ref, out_ref, held_ref, made_ref, sems):
    def fetch(k):
        dist, slot = sel_ref[k], k % 2
        return pltpu.make_async_copy(tiles_ref.at[:, dist], held_ref.at[slot], sems.at[0, slot])

    def store(k):
        return pltpu.make_async_copy(made_ref.at[k % 2], out_ref.at[k], sems.at[1, k % 2])

    fetch(0).start()
    for k in range(n):
        fetch(k).wait()
        if k + 1 < n:
            fetch(k + 1).start()
        if k > 1:
            store(k - 2).wait()
        dist, slot = sel_ref[k], k % 2

        def block_row(b, carry):
            count = counts_ref[b * ND + dist]
            rows = pl.ds(pl.multiple_of(b * BS, BS), BS)
            cols = [cols_ref[(b * ND + dist) * NS + s] for s in range(NS)]
            cols = [jnp.where(s < count, cols[s], NB) for s in range(NS)]
            tiles = [held_ref[slot, b, s] for s in range(NS)]
            zero = jnp.zeros((BS, BS), jnp.bfloat16)
            for c in range(NB):
                parts = [jnp.where(cols[s] == c, tiles[s], zero) for s in range(NS)]
                pairs = [parts[s] + parts[s + 1] for s in range(0, NS, 2)]
                made_ref[slot, c, rows, :] = pairs[0] + pairs[1] + pairs[2]
            return carry

        lax.fori_loop(0, NB, block_row, 0)
        store(k).start()
    store(n - 2).wait()
    store(n - 1).wait()


def assemble_call(sel, cols, counts, tiles):
    n = sel.shape[0]
    return pl.pallas_call(
        functools.partial(assemble_body, n),
        out_shape=jax.ShapeDtypeStruct((n, NB, NB * BS, BS), jnp.bfloat16),
        in_specs=[SMEM] * 3 + [HBM],
        out_specs=HBM,
        scratch_shapes=[
            pltpu.VMEM((2, NB, NS, BS, BS), jnp.bfloat16),
            pltpu.VMEM((2, NB, NB * BS, BS), jnp.bfloat16),
            pltpu.SemaphoreType.DMA((2, 2)),
        ],
        compiler_params=params(),
        cost_estimate=matmul_cost(n),
        name="assemble_adjacency",
    )(sel, cols, counts, tiles)


def copies_of(adj_ref, places, held_ref, sems):
    copies = [
        pltpu.make_async_copy(adj_ref.at[place], held_ref.at[k], sems.at[k])
        for k, place in enumerate(places)
    ]
    for copy in copies:
        copy.start()
    return copies


def copy_scratch(n):
    return [
        pltpu.VMEM((n, NB, NB * BS, BS), jnp.bfloat16),
        pltpu.SemaphoreType.DMA((n,)),
    ]


def wide(ref, k):
    return jnp.concatenate([ref[k, c] for c in range(NB)], 1)


def forward_body(n, start, first, last, core_ref, adj_ref, *refs):
    shards, rest = refs[:n], refs[n:]
    total_ref, held_ref, sems = rest[-3:]
    outs = rest[-5:-3] if last else rest[-4:-3]
    copies = copies_of(adj_ref, range(start, start + n), held_ref, sems)
    for k in range(n):
        copies[k].wait()
        product = jnp.dot(wide(held_ref, k), shards[k][...], preferred_element_type=jnp.float32)
        if k > 0:
            total_ref[...] += product
        else:
            total_ref[...] = product if first else rest[0][...] + product
    if last:
        core = core_ref[0]
        for part in range(2):
            keep = pl.multiple_of((part * 2 + core) * 256, 256)
            away = pl.multiple_of((part * 2 + 1 - core) * 256, 256)
            outs[0][part] = total_ref[pl.ds(keep, 256), :]
            outs[1][part] = total_ref[pl.ds(away, 256), :].astype(jnp.bfloat16)
    else:
        outs[0][...] = total_ref[...]


def forward_call(core, adjacency, start, shards, before, last, after):
    n, first = len(shards), before is None
    if last:
        out_shape = (
            jax.ShapeDtypeStruct((2, 256, F), jnp.float32),
            jax.ShapeDtypeStruct((2, 256, F), jnp.bfloat16),
        )
    else:
        out_shape = (jax.ShapeDtypeStruct((NB * BS, F), jnp.float32),)
    return pl.pallas_call(
        functools.partial(forward_body, n, start, first, last),
        out_shape=out_shape,
        in_specs=[SMEM, HBM] + [WHOLE] * (n + (not first)) + [UNREAD] * len(after),
        out_specs=(WHOLE,) * len(out_shape),
        scratch_shapes=[pltpu.VMEM((NB * BS, F), jnp.float32)] + copy_scratch(n),
        compiler_params=params(),
        cost_estimate=matmul_cost(n),
        name="forward_product",
    )(core, adjacency, *shards, *([] if first else [before]), *after)


def dense_body(
    rep_ref, own_ref, got_ref, feat_ref, cot_ref, inv_ref, ws_ref, wn_ref, bias_ref,
    act_ref, term_ref, back_ref, grad_ref,
):
    zh = rep_ref[0] // 2
    nt = (((1,), (1,)), ((), ()))
    tn = (((0,), (0,)), ((), ()))
    grads = jnp.zeros((F, F), jnp.float32)
    sums = jnp.zeros((1, F), jnp.float32)
    for part in range(2):
        feat = feat_ref[part]
        inv = inv_ref[part]
        summed = own_ref[part].astype(jnp.float32) + got_ref[part].astype(jnp.float32)
        agg = (summed * jnp.broadcast_to(inv, (256, 256)).T).astype(jnp.bfloat16)
        pre = (
            jnp.dot(feat, ws_ref[...], preferred_element_type=jnp.float32)
            + jnp.dot(agg, wn_ref[...], preferred_element_type=jnp.float32)
            + bias_ref[...]
        )
        sigm = jax.nn.sigmoid(pre)
        act = (pre * sigm).astype(jnp.bfloat16)
        slope = sigm * (1.0 + pre * (1.0 - sigm))
        grad_pre = (cot_ref[part].astype(jnp.float32) * slope).astype(jnp.bfloat16)

        @pl.when(zh == part)
        def _():
            act_ref[...] = act
            term_ref[...] = lax.dot_general(
                grad_pre, ws_ref[...], nt, preferred_element_type=jnp.float32
            )

        back_t = lax.dot_general(wn_ref[...], grad_pre, nt, preferred_element_type=jnp.float32)
        back_ref[part] = (back_t * inv).astype(jnp.bfloat16)
        left = jnp.where(zh == 0, feat, agg)
        grads += lax.dot_general(left, grad_pre, tn, preferred_element_type=jnp.float32)
        sums += jnp.sum(grad_pre.astype(jnp.float32), axis=0, keepdims=True)
    grad_ref[:F, :] = grads
    grad_ref[F:, :] = jnp.broadcast_to(sums, (8, F))


def dense_call(rep, own, got, feat, cot, inv, w_self, w_neigh, bias):
    return pl.pallas_call(
        dense_body,
        out_shape=(
            jax.ShapeDtypeStruct((256, F), jnp.bfloat16),
            jax.ShapeDtypeStruct((256, F), jnp.float32),
            jax.ShapeDtypeStruct((2, F, 256), jnp.bfloat16),
            jax.ShapeDtypeStruct((F + 8, F), jnp.float32),
        ),
        in_specs=[SMEM] + [WHOLE] * 8,
        out_specs=(WHOLE,) * 4,
        compiler_params=params(SMALL),
        name="dense_rows",
    )(rep, own, got, feat, cot, inv, w_self, w_neigh, bias)


def backward_body(places, added, core_ref, adj_ref, own_ref, got_ref, *rest):
    n = len(places)
    held_ref, sems = rest[-2:]
    outs = rest[-2 - n : -2]
    copies = copies_of(adj_ref, places, held_ref, sems)
    core = core_ref[0]
    message = []
    for quarter in range(4):
        mine = core == quarter % 2
        message.append(jnp.where(mine, own_ref[quarter // 2], got_ref[quarter // 2]))
    message = jnp.concatenate(message, 1)
    for k in range(n):
        copies[k].wait()
        product = jnp.dot(message, wide(held_ref, k), preferred_element_type=jnp.float32)
        for c in range(NB):
            part = product[:, c * BS : (c + 1) * BS]
            for ref in rest[:added]:
                part += ref[c].astype(jnp.float32)
            outs[k][c] = part.astype(jnp.bfloat16)


def backward_call(core, adjacency, places, own, got, extra, after):
    n, added = len(places), len(extra)
    return pl.pallas_call(
        functools.partial(backward_body, tuple(places), added),
        out_shape=(jax.ShapeDtypeStruct((NB, F, BS), jnp.bfloat16),) * n,
        in_specs=[SMEM, HBM] + [WHOLE] * (2 + added) + [UNREAD] * len(after),
        out_specs=(WHOLE,) * n,
        scratch_shapes=copy_scratch(n),
        compiler_params=params(),
        cost_estimate=matmul_cost(n),
        name="backward_product",
    )(core, adjacency, own, got, *extra, *after)


def split_body(core_ref, *rest):
    arrived, (keep_ref, away_ref) = rest[:-2], rest[-2:]
    core = core_ref[0]
    for part in range(2):
        for c in range(2):
            keep = (part * 2 + core) * 2 + c
            away = (part * 2 + 1 - core) * 2 + c
            kept = arrived[0][keep].astype(jnp.float32)
            sent = arrived[0][away].astype(jnp.float32)
            for ref in arrived[1:]:
                kept += ref[keep].astype(jnp.float32)
                sent += ref[away].astype(jnp.float32)
            keep_ref[part, c] = kept
            away_ref[part, c] = sent.astype(jnp.bfloat16)


def split_call(core, arrived):
    return pl.pallas_call(
        split_body,
        out_shape=(
            jax.ShapeDtypeStruct((2, 2, F, BS), jnp.float32),
            jax.ShapeDtypeStruct((2, 2, F, BS), jnp.bfloat16),
        ),
        in_specs=[SMEM] + [WHOLE] * len(arrived),
        out_specs=(WHOLE, WHOLE),
        compiler_params=params(SMALL),
        name="split_products",
    )(core, *arrived)


def hold_body(*refs):
    pass


def hold_call(along, after):
    return pl.pallas_call(
        hold_body,
        out_shape=jax.ShapeDtypeStruct(along.shape, along.dtype),
        in_specs=[UNREAD] * (1 + len(after)),
        out_specs=UNREAD,
        input_output_aliases={0: 0},
        name="hold",
    )(along, *after)


def merge_body(zh_ref, kept_ref, got_ref, mine_ref, sent_ref):
    zh = zh_ref[0]
    mine_ref[...] = kept_ref[zh] + got_ref[zh].astype(jnp.float32)
    sent = kept_ref[1 - zh] + got_ref[1 - zh].astype(jnp.float32)
    sent_ref[...] = sent.astype(jnp.bfloat16)


def merge_call(zh, kept, got):
    return pl.pallas_call(
        merge_body,
        out_shape=(
            jax.ShapeDtypeStruct((2, F, BS), jnp.float32),
            jax.ShapeDtypeStruct((2, F, BS), jnp.bfloat16),
        ),
        in_specs=[SMEM, WHOLE, WHOLE],
        out_specs=(WHOLE, WHOLE),
        compiler_params=params(SMALL),
        name="merge_products",
    )(zh, kept, got)


def final_body(kept_ref, got_ref, term_ref, out_ref):
    for c in range(2):
        spread = kept_ref[c] + got_ref[c].astype(jnp.float32)
        rows = slice(c * BS, (c + 1) * BS)
        out_ref[rows, :] = (term_ref[rows, :] + spread.T).astype(jnp.bfloat16)


def final_call(kept, got, term):
    return pl.pallas_call(
        final_body,
        out_shape=jax.ShapeDtypeStruct((256, F), jnp.bfloat16),
        compiler_params=params(SMALL),
        name="final_rows",
    )(kept, got, term)


def pick(pair, index):
    return lax.dynamic_index_in_dim(pair, index, 0, keepdims=False)


def weight_shares(grads, core):
    halves, sums = grads[:F].reshape(2, F // 2, F), grads[F:]
    away = jnp.concatenate([pick(halves, 1 - core), sums], 0)
    mine = jnp.concatenate([pick(halves, core), sums], 0) + send(away, flip_pairs(dcore=1))
    count = lax.axis_size("blk")
    bias = mine[F // 2 : F // 2 + 1]
    high = bias.astype(jnp.bfloat16)
    low = (bias - high.astype(jnp.float32)).astype(jnp.bfloat16)
    bias_rows = jnp.broadcast_to(jnp.concatenate([high, low], 0)[None], (count, 2, F))
    rows = mine[: F // 2].astype(jnp.bfloat16).reshape(count, F // 2 // count, F)
    return lax.all_to_all(jnp.concatenate([rows, bias_rows], 1), "blk", 0, 0)


def weight_grads(parts, zh, core, nodes):
    count, share = parts.shape[0], parts.shape[1] - 2
    total = jnp.sum(parts.astype(jnp.float32), axis=0)
    bias = total[share] + total[share + 1]
    spread = jnp.broadcast_to(total[None, :share], (count, share, F))
    half = lax.all_to_all(spread, "blk", 0, 0).reshape(F // 2, F)
    other = send(half, flip_pairs(dzh=1))
    both = jnp.where(zh == 0, jnp.stack([half, other]), jnp.stack([other, half]))
    across = send(both, flip_pairs(dcore=1))
    low, top = jnp.where(core == 0, both, across), jnp.where(core == 0, across, both)
    norm = 1.0 / jnp.sqrt(jnp.float32(nodes))
    whole = jnp.concatenate([low, top], 1) * norm
    return whole[0], whole[1], bias * norm


def shards(
    features, tiles, tile_cols, counts, degree, train_mask, cotangent, w_self, w_neigh, bias_term
):
    rows = features.shape[0]
    rep = lax.axis_index("rep").astype(jnp.int32)
    zh, core = rep // 2, rep % 2
    place = (lax.axis_index("blk") % 8).astype(jnp.int32)
    cols = tile_cols.reshape(-1)
    live = counts.reshape(-1)

    def distance_of(k):
        return (place - (place ^ k)) % 8

    def own_rows(value):
        value = value.reshape((2, 2, rows // 4) + value.shape[1:])
        return lax.dynamic_index_in_dim(value, core, 1, keepdims=False)

    inv = own_rows(1.0 / degree.astype(jnp.float32))[:, None, :]
    feat = own_rows(features)
    cot = own_rows(cotangent) * own_rows(train_mask).astype(jnp.bfloat16)[:, :, None]
    bias = bias_term.reshape(1, F)

    order = list(PLAN)
    sel = jnp.stack([distance_of(k) for k in order])
    adjacency = assemble_call(sel, cols, live, tiles)
    blocks, held = {}, []
    for k, via in PLAN.items():
        if via is None:
            blocks[k] = send(features, column_pairs(k, PLAN, CROSS))
    for k, after in HELD:
        blocks[k] = hold_call(blocks[k], [adjacency] + [blocks[a] for a in after])
        held.append(blocks[k])
    for k, via in PLAN.items():
        if via is not None:
            blocks[k] = send(blocks[k ^ via], column_pairs(k, PLAN, CROSS))
    made = (None,)
    for group in GROUPS:
        made = forward_call(
            core[None],
            adjacency,
            order.index(group[0]),
            [blocks[k] for k in group],
            made[0],
            group is GROUPS[-1],
            held if group is GROUPS[0] else [],
        )

    kept, away = made
    chip = (kept + send(away, flip_pairs(dcore=1)).astype(jnp.float32)).astype(jnp.bfloat16)
    other = send(chip, flip_pairs(dzh=1))

    activation, own_term, back_own, grads = dense_call(
        rep[None], chip, other, feat, cot, inv, w_self, w_neigh, bias
    )
    back_got = send(back_own, flip_pairs(dcore=1))

    parts = weight_shares(grads, core)
    arrived, extra = {}, {}
    for group in BACK:
        made = backward_call(
            core[None],
            adjacency,
            [order.index(k) for k in group],
            back_own,
            back_got,
            extra.get(group[0], []),
            [parts] if group[0] in LATER else [],
        )
        for k, product in zip(group, made):
            pairs = column_pairs(k, BACK_PLAN, BACK_CROSS)
            moved = send(product, [(b, a) for a, b in pairs])
            if BACK_PLAN[k] is None:
                arrived[k] = moved
            else:
                extra.setdefault(k ^ BACK_PLAN[k], []).append(moved)
    kept, away = split_call(core[None], list(arrived.values()))
    mine, sent = merge_call(zh[None], kept, send(away, flip_pairs(dcore=1)))
    grad_features = final_call(mine, send(sent, flip_pairs(dzh=1)), own_term)
    grad_self, grad_neigh, grad_bias = weight_grads(
        parts, zh, core, rows * lax.axis_size("blk")
    )
    return (activation, grad_features, grad_self, grad_neigh, grad_bias)


def solution(mesh):
    return jax.shard_map(
        shards,
        mesh=mesh,
        in_specs=(
            P("blk", None),
            P("blk", "rep", None, None, None),
            P("blk", "rep", None),
            P("blk", "rep"),
            P("blk"),
            P("blk"),
            P("blk", None),
            P(),
            P(),
            P(),
        ),
        out_specs=(P(("blk", "rep"), None), P(("blk", "rep"), None), P(), P(), P()),
        check_vma=False,
    )
```

```python
import functools

import jax
import jax.numpy as jnp
from jax import lax
from jax.experimental import pallas as pl
from jax.experimental.pallas import tpu as pltpu
from jax.sharding import PartitionSpec as P

AXES = ("blk", "rep")
NB = 8
ND = 8
NS = 6
BS = 128
F = 256
VMEM = 50 * 1024 * 1024
SMALL = 16 * 1024 * 1024
PLAN = {6: None, 3: None, 1: None, 2: None, 0: None, 7: 1, 4: 2, 5: 6}
CROSS = {1: 0x7666, 3: 0x5FDB}
BACK_PLAN = {6: None, 1: None, 0: None, 2: 2, 3: 1, 7: 1, 4: 2, 5: 2}
BACK_CROSS = {1: 0xAAAA}
GROUPS = ((6, 3, 1, 2, 0), (7, 4, 5))
HELD = ((6, (1,)), (3, (2, 0)))
BACK = ((5, 3, 4, 1), (7,), (2,), (6,), (0,))
LATER = (2,)
AFTER = {6: (1,)}


def index_of(y, x, zl, zh, core):
    return (((y % 4 * 4 + x % 4) * 2 + zl) * 2 + zh) * 2 + core


def places():
    for t in range(128):
        yield t, t >> 5, t >> 3 & 3, t >> 2 & 1, t >> 1 & 1, t & 1


def column_pairs(k, plan, cross):
    via = plan[k]
    out = []
    for t, y, x, zl, zh, core in places():
        j, r = x * 2 + zl, 2 * zh + core
        jj = j ^ k
        if via is None:
            flip = cross[k] >> (jj * 2 + core) & 1 if k & 1 else 0
            out.append((index_of(y - r - (jj > j), jj >> 1, jj & 1, zh ^ flip, core), t))
        else:
            jn = j ^ via
            out.append((index_of(y - (jj > j) + (jj > jn), jn >> 1, jn & 1, zh, core), t))
    return out


def flip_pairs(dy=0, dx=0, dzl=0, dzh=0, dcore=0):
    return [
        (t, index_of(y ^ dy, x ^ dx, zl ^ dzl, zh ^ dzh, core ^ dcore))
        for t, y, x, zl, zh, core in places()
    ]


def send(value, pairs):
    return lax.ppermute(value, AXES, pairs)


def params(limit=VMEM):
    return pltpu.CompilerParams(vmem_limit_bytes=limit)


SMEM = pl.BlockSpec(memory_space=pltpu.SMEM)
HBM = pl.BlockSpec(memory_space=pltpu.HBM)
UNREAD = pl.BlockSpec(memory_space=pl.ANY)
WHOLE = pl.BlockSpec(memory_space=pltpu.VMEM)


def matmul_cost(n):
    return pl.CostEstimate(
        flops=2 * NB * NB * BS * BS * F * n, bytes_accessed=(3 << 20) * n, transcendentals=0
    )


def assemble_body(n, sel_ref, cols_ref, counts_ref, tiles_ref, out_ref, held_ref, made_ref, sems):
    def fetch(k):
        dist, slot = sel_ref[k], k % 2
        return pltpu.make_async_copy(tiles_ref.at[:, dist], held_ref.at[slot], sems.at[0, slot])

    def store(k):
        return pltpu.make_async_copy(made_ref.at[k % 2], out_ref.at[k], sems.at[1, k % 2])

    fetch(0).start()
    for k in range(n):
        fetch(k).wait()
        if k + 1 < n:
            fetch(k + 1).start()
        if k > 1:
            store(k - 2).wait()
        dist, slot = sel_ref[k], k % 2

        def block_row(b, carry):
            count = counts_ref[b * ND + dist]
            rows = pl.ds(pl.multiple_of(b * BS, BS), BS)
            cols = [cols_ref[(b * ND + dist) * NS + s] for s in range(NS)]
            cols = [jnp.where(s < count, cols[s], NB) for s in range(NS)]
            tiles = [held_ref[slot, b, s] for s in range(NS)]
            zero = jnp.zeros((BS, BS), jnp.bfloat16)
            for c in range(NB):
                parts = [jnp.where(cols[s] == c, tiles[s], zero) for s in range(NS)]
                pairs = [parts[s] + parts[s + 1] for s in range(0, NS, 2)]
                made_ref[slot, c, rows, :] = pairs[0] + pairs[1] + pairs[2]
            return carry

        lax.fori_loop(0, NB, block_row, 0)
        store(k).start()
    store(n - 2).wait()
    store(n - 1).wait()


def assemble_call(sel, cols, counts, tiles):
    n = sel.shape[0]
    return pl.pallas_call(
        functools.partial(assemble_body, n),
        out_shape=jax.ShapeDtypeStruct((n, NB, NB * BS, BS), jnp.bfloat16),
        in_specs=[SMEM] * 3 + [HBM],
        out_specs=HBM,
        scratch_shapes=[
            pltpu.VMEM((2, NB, NS, BS, BS), jnp.bfloat16),
            pltpu.VMEM((2, NB, NB * BS, BS), jnp.bfloat16),
            pltpu.SemaphoreType.DMA((2, 2)),
        ],
        compiler_params=params(),
        cost_estimate=matmul_cost(n),
        name="assemble_adjacency",
    )(sel, cols, counts, tiles)


def copies_of(adj_ref, places, held_ref, sems):
    copies = [
        pltpu.make_async_copy(adj_ref.at[place], held_ref.at[k], sems.at[k])
        for k, place in enumerate(places)
    ]
    for copy in copies:
        copy.start()
    return copies


def copy_scratch(n):
    return [
        pltpu.VMEM((n, NB, NB * BS, BS), jnp.bfloat16),
        pltpu.SemaphoreType.DMA((n,)),
    ]


def wide(ref, k):
    return jnp.concatenate([ref[k, c] for c in range(NB)], 1)


def forward_body(n, start, first, last, core_ref, adj_ref, *refs):
    shards, rest = refs[:n], refs[n:]
    total_ref, held_ref, sems = rest[-3:]
    outs = rest[-5:-3] if last else rest[-4:-3]
    copies = copies_of(adj_ref, range(start, start + n), held_ref, sems)
    for k in range(n):
        copies[k].wait()
        product = jnp.dot(wide(held_ref, k), shards[k][...], preferred_element_type=jnp.float32)
        if k > 0:
            total_ref[...] += product
        else:
            total_ref[...] = product if first else rest[0][...] + product
    if last:
        core = core_ref[0]
        for part in range(2):
            keep = pl.multiple_of((part * 2 + core) * 256, 256)
            away = pl.multiple_of((part * 2 + 1 - core) * 256, 256)
            outs[0][part] = total_ref[pl.ds(keep, 256), :]
            outs[1][part] = total_ref[pl.ds(away, 256), :].astype(jnp.bfloat16)
    else:
        outs[0][...] = total_ref[...]


def forward_call(core, adjacency, start, shards, before, last, after):
    n, first = len(shards), before is None
    if last:
        out_shape = (
            jax.ShapeDtypeStruct((2, 256, F), jnp.float32),
            jax.ShapeDtypeStruct((2, 256, F), jnp.bfloat16),
        )
    else:
        out_shape = (jax.ShapeDtypeStruct((NB * BS, F), jnp.float32),)
    return pl.pallas_call(
        functools.partial(forward_body, n, start, first, last),
        out_shape=out_shape,
        in_specs=[SMEM, HBM] + [WHOLE] * (n + (not first)) + [UNREAD] * len(after),
        out_specs=(WHOLE,) * len(out_shape),
        scratch_shapes=[pltpu.VMEM((NB * BS, F), jnp.float32)] + copy_scratch(n),
        compiler_params=params(),
        cost_estimate=matmul_cost(n),
        name="forward_product",
    )(core, adjacency, *shards, *([] if first else [before]), *after)


def dense_body(
    rep_ref, own_ref, got_ref, feat_ref, cot_ref, inv_ref, ws_ref, wn_ref, bias_ref,
    act_ref, term_ref, back_ref, grad_ref,
):
    zh = rep_ref[0] // 2
    nt = (((1,), (1,)), ((), ()))
    tn = (((0,), (0,)), ((), ()))
    grads = jnp.zeros((F, F), jnp.float32)
    sums = jnp.zeros((1, F), jnp.float32)
    for part in range(2):
        feat = feat_ref[part]
        inv = inv_ref[part]
        summed = own_ref[part].astype(jnp.float32) + got_ref[part].astype(jnp.float32)
        agg = (summed * jnp.broadcast_to(inv, (256, 256)).T).astype(jnp.bfloat16)
        pre = (
            jnp.dot(feat, ws_ref[...], preferred_element_type=jnp.float32)
            + jnp.dot(agg, wn_ref[...], preferred_element_type=jnp.float32)
            + bias_ref[...]
        )
        sigm = jax.nn.sigmoid(pre)
        act = (pre * sigm).astype(jnp.bfloat16)
        slope = sigm * (1.0 + pre * (1.0 - sigm))
        grad_pre = (cot_ref[part].astype(jnp.float32) * slope).astype(jnp.bfloat16)

        @pl.when(zh == part)
        def _():
            act_ref[...] = act
            term_ref[...] = lax.dot_general(
                grad_pre, ws_ref[...], nt, preferred_element_type=jnp.float32
            )

        back_t = lax.dot_general(wn_ref[...], grad_pre, nt, preferred_element_type=jnp.float32)
        back_ref[part] = (back_t * inv).astype(jnp.bfloat16)
        left = jnp.where(zh == 0, feat, agg)
        grads += lax.dot_general(left, grad_pre, tn, preferred_element_type=jnp.float32)
        sums += jnp.sum(grad_pre.astype(jnp.float32), axis=0, keepdims=True)
    grad_ref[:F, :] = grads
    grad_ref[F:, :] = jnp.broadcast_to(sums, (8, F))


def dense_call(rep, own, got, feat, cot, inv, w_self, w_neigh, bias):
    return pl.pallas_call(
        dense_body,
        out_shape=(
            jax.ShapeDtypeStruct((256, F), jnp.bfloat16),
            jax.ShapeDtypeStruct((256, F), jnp.float32),
            jax.ShapeDtypeStruct((2, F, 256), jnp.bfloat16),
            jax.ShapeDtypeStruct((F + 8, F), jnp.float32),
        ),
        in_specs=[SMEM] + [WHOLE] * 8,
        out_specs=(WHOLE,) * 4,
        compiler_params=params(SMALL),
        name="dense_rows",
    )(rep, own, got, feat, cot, inv, w_self, w_neigh, bias)


def backward_body(places, added, core_ref, adj_ref, own_ref, got_ref, *rest):
    n = len(places)
    held_ref, sems = rest[-2:]
    outs = rest[-2 - n : -2]
    copies = copies_of(adj_ref, places, held_ref, sems)
    core = core_ref[0]
    message = []
    for quarter in range(4):
        mine = core == quarter % 2
        message.append(jnp.where(mine, own_ref[quarter // 2], got_ref[quarter // 2]))
    message = jnp.concatenate(message, 1)
    for k in range(n):
        copies[k].wait()
        product = jnp.dot(message, wide(held_ref, k), preferred_element_type=jnp.float32)
        for c in range(NB):
            part = product[:, c * BS : (c + 1) * BS]
            for ref in rest[:added]:
                part += ref[c].astype(jnp.float32)
            outs[k][c] = part.astype(jnp.bfloat16)


def backward_call(core, adjacency, places, own, got, extra, after):
    n, added = len(places), len(extra)
    return pl.pallas_call(
        functools.partial(backward_body, tuple(places), added),
        out_shape=(jax.ShapeDtypeStruct((NB, F, BS), jnp.bfloat16),) * n,
        in_specs=[SMEM, HBM] + [WHOLE] * (2 + added) + [UNREAD] * len(after),
        out_specs=(WHOLE,) * n,
        scratch_shapes=copy_scratch(n),
        compiler_params=params(),
        cost_estimate=matmul_cost(n),
        name="backward_product",
    )(core, adjacency, own, got, *extra, *after)


def split_body(core_ref, *rest):
    arrived, (keep_ref, away_ref) = rest[:-2], rest[-2:]
    core = core_ref[0]
    for part in range(2):
        for c in range(2):
            keep = (part * 2 + core) * 2 + c
            away = (part * 2 + 1 - core) * 2 + c
            kept = arrived[0][keep].astype(jnp.float32)
            sent = arrived[0][away].astype(jnp.float32)
            for ref in arrived[1:]:
                kept += ref[keep].astype(jnp.float32)
                sent += ref[away].astype(jnp.float32)
            keep_ref[part, c] = kept
            away_ref[part, c] = sent.astype(jnp.bfloat16)


def split_call(core, arrived):
    return pl.pallas_call(
        split_body,
        out_shape=(
            jax.ShapeDtypeStruct((2, 2, F, BS), jnp.float32),
            jax.ShapeDtypeStruct((2, 2, F, BS), jnp.bfloat16),
        ),
        in_specs=[SMEM] + [WHOLE] * len(arrived),
        out_specs=(WHOLE, WHOLE),
        compiler_params=params(SMALL),
        name="split_products",
    )(core, *arrived)


def hold_body(*refs):
    pass


def hold_call(along, after):
    return pl.pallas_call(
        hold_body,
        out_shape=jax.ShapeDtypeStruct(along.shape, along.dtype),
        in_specs=[UNREAD] * (1 + len(after)),
        out_specs=UNREAD,
        input_output_aliases={0: 0},
        name="hold",
    )(along, *after)


def merge_body(zh_ref, kept_ref, got_ref, mine_ref, sent_ref):
    zh = zh_ref[0]
    mine_ref[...] = kept_ref[zh] + got_ref[zh].astype(jnp.float32)
    sent = kept_ref[1 - zh] + got_ref[1 - zh].astype(jnp.float32)
    sent_ref[...] = sent.astype(jnp.bfloat16)


def merge_call(zh, kept, got):
    return pl.pallas_call(
        merge_body,
        out_shape=(
            jax.ShapeDtypeStruct((2, F, BS), jnp.float32),
            jax.ShapeDtypeStruct((2, F, BS), jnp.bfloat16),
        ),
        in_specs=[SMEM, WHOLE, WHOLE],
        out_specs=(WHOLE, WHOLE),
        compiler_params=params(SMALL),
        name="merge_products",
    )(zh, kept, got)


def final_body(kept_ref, got_ref, term_ref, out_ref):
    for c in range(2):
        spread = kept_ref[c] + got_ref[c].astype(jnp.float32)
        rows = slice(c * BS, (c + 1) * BS)
        out_ref[rows, :] = (term_ref[rows, :] + spread.T).astype(jnp.bfloat16)


def final_call(kept, got, term):
    return pl.pallas_call(
        final_body,
        out_shape=jax.ShapeDtypeStruct((256, F), jnp.bfloat16),
        compiler_params=params(SMALL),
        name="final_rows",
    )(kept, got, term)


def pick(pair, index):
    return lax.dynamic_index_in_dim(pair, index, 0, keepdims=False)


def weight_shares(grads, core):
    halves, sums = grads[:F].reshape(2, F // 2, F), grads[F:]
    away = jnp.concatenate([pick(halves, 1 - core), sums], 0)
    mine = jnp.concatenate([pick(halves, core), sums], 0) + send(away, flip_pairs(dcore=1))
    count = lax.axis_size("blk")
    bias = mine[F // 2 : F // 2 + 1]
    high = bias.astype(jnp.bfloat16)
    low = (bias - high.astype(jnp.float32)).astype(jnp.bfloat16)
    bias_rows = jnp.broadcast_to(jnp.concatenate([high, low], 0)[None], (count, 2, F))
    rows = mine[: F // 2].astype(jnp.bfloat16).reshape(count, F // 2 // count, F)
    return lax.all_to_all(jnp.concatenate([rows, bias_rows], 1), "blk", 0, 0)


def weight_grads(parts, zh, core, nodes):
    count, share = parts.shape[0], parts.shape[1] - 2
    total = jnp.sum(parts.astype(jnp.float32), axis=0)
    bias = total[share] + total[share + 1]
    spread = jnp.broadcast_to(total[None, :share], (count, share, F))
    half = lax.all_to_all(spread, "blk", 0, 0).reshape(F // 2, F)
    other = send(half, flip_pairs(dzh=1))
    both = jnp.where(zh == 0, jnp.stack([half, other]), jnp.stack([other, half]))
    across = send(both, flip_pairs(dcore=1))
    low, top = jnp.where(core == 0, both, across), jnp.where(core == 0, across, both)
    norm = 1.0 / jnp.sqrt(jnp.float32(nodes))
    whole = jnp.concatenate([low, top], 1) * norm
    return whole[0], whole[1], bias * norm


def shards(
    features, tiles, tile_cols, counts, degree, train_mask, cotangent, w_self, w_neigh, bias_term
):
    rows = features.shape[0]
    rep = lax.axis_index("rep").astype(jnp.int32)
    zh, core = rep // 2, rep % 2
    place = (lax.axis_index("blk") % 8).astype(jnp.int32)
    cols = tile_cols.reshape(-1)
    live = counts.reshape(-1)

    def distance_of(k):
        return (place - (place ^ k)) % 8

    def own_rows(value):
        value = value.reshape((2, 2, rows // 4) + value.shape[1:])
        return lax.dynamic_index_in_dim(value, core, 1, keepdims=False)

    inv = own_rows(1.0 / degree.astype(jnp.float32))[:, None, :]
    feat = own_rows(features)
    cot = own_rows(cotangent) * own_rows(train_mask).astype(jnp.bfloat16)[:, :, None]
    bias = bias_term.reshape(1, F)

    order = list(PLAN)
    sel = jnp.stack([distance_of(k) for k in order])
    adjacency = assemble_call(sel, cols, live, tiles)
    blocks, held = {}, []
    for k, via in PLAN.items():
        if via is None:
            blocks[k] = send(features, column_pairs(k, PLAN, CROSS))
    for k, after in HELD:
        blocks[k] = hold_call(blocks[k], [adjacency] + [blocks[a] for a in after])
        held.append(blocks[k])
    for k, via in PLAN.items():
        if via is not None:
            blocks[k] = send(blocks[k ^ via], column_pairs(k, PLAN, CROSS))
    made = (None,)
    for group in GROUPS:
        made = forward_call(
            core[None],
            adjacency,
            order.index(group[0]),
            [blocks[k] for k in group],
            made[0],
            group is GROUPS[-1],
            held if group is GROUPS[0] else [],
        )

    kept, away = made
    chip = (kept + send(away, flip_pairs(dcore=1)).astype(jnp.float32)).astype(jnp.bfloat16)
    other = send(chip, flip_pairs(dzh=1))

    activation, own_term, back_own, grads = dense_call(
        rep[None], chip, other, feat, cot, inv, w_self, w_neigh, bias
    )
    back_got = send(back_own, flip_pairs(dcore=1))

    parts = weight_shares(grads, core)
    arrived, extra = {}, {}
    for group in BACK:
        made = backward_call(
            core[None],
            adjacency,
            [order.index(k) for k in group],
            back_own,
            back_got,
            extra.get(group[0], []),
            [parts] if group[0] in LATER else [arrived[k] for k in AFTER.get(group[0], ())],
        )
        for k, product in zip(group, made):
            pairs = column_pairs(k, BACK_PLAN, BACK_CROSS)
            moved = send(product, [(b, a) for a, b in pairs])
            if BACK_PLAN[k] is None:
                arrived[k] = moved
            else:
                extra.setdefault(k ^ BACK_PLAN[k], []).append(moved)
    kept, away = split_call(core[None], list(arrived.values()))
    mine, sent = merge_call(zh[None], kept, send(away, flip_pairs(dcore=1)))
    grad_features = final_call(mine, send(sent, flip_pairs(dzh=1)), own_term)
    grad_self, grad_neigh, grad_bias = weight_grads(
        parts, zh, core, rows * lax.axis_size("blk")
    )
    return (activation, grad_features, grad_self, grad_neigh, grad_bias)


def solution(mesh):
    return jax.shard_map(
        shards,
        mesh=mesh,
        in_specs=(
            P("blk", None),
            P("blk", "rep", None, None, None),
            P("blk", "rep", None),
            P("blk", "rep"),
            P("blk"),
            P("blk"),
            P("blk", None),
            P(),
            P(),
            P(),
        ),
        out_specs=(P(("blk", "rep"), None), P(("blk", "rep"), None), P(), P(), P()),
        check_vma=False,
    )
```
